256 devices in a mesh: blk: 128 (over z, x_lo, y, core), seg: 2 (over x_hi).
Axes of the slice: x: 4 (x_hi: 2, x_lo: 2; x = x_hi * 2 + x_lo), y: 4, z: 8, core: 2. Of those that a mesh axis runs over, the one named last changes fastest.
Arguments:
- spectra: bfloat16 [8, 8192, 2, 2048], P('seg', 'blk'), may hold values from -3000 to 3000
- owner_device: int32 [524288, 1], P('blk'), may hold values from 0 to 127; in each aligned block of 4096 rows (0 to 4095, 4096 to 8191, ...) at most 64 rows name the same one
- stack_slot: int32 [524288], P('blk'), may hold values from 0 to 127
Outputs:
- stacks: bfloat16 [16384, 512], P('blk', 'seg')
The draws below stay inside these ranges and needn't reach their ends.
Inputs may be any that keep to these rules, and one draw needn't show every extreme that they name: `owner_device`: among the 4096 rows of one block and round (aligned blocks of rows) at most 64 name the same owner, and exactly 64 in some of them.
All inputs are finite; a program needn't handle non-finite values.
Results may differ from the reference program's by a relative error of at most 0.0034.
Values may be sent and summed in bfloat16 or wider, within the bound.
A program may use at most 64 MiB of HBM per device.

```python
import math
import jax
import jax.numpy as jnp
import numpy as np
from jax import lax

CB = 64
SEG_DEV = 4
F = 2048
NFFT = 16384
LAGS = 512
WBAND = 128
ROUNDS = 1
STACKS_DEV = 128
PAIRS = 4096
CAP = 64
CHANNELS = 8192
SEGMENTS = 8
STACKS = 16384
ROWS = 524288
N_BLK = 128
N_SEG = 2


def draw_spectra(key, part):
    key = jax.random.fold_in(key, 11)
    first, second, third, fourth = jax.random.split(key, 4)
    shape = (SEGMENTS, CHANNELS, 2, F)
    channel_scale = jnp.exp(jax.random.uniform(second, (1, CHANNELS, 1, 1), jnp.float32, 0.0, math.log(10.0)))
    bin_scale = jnp.exp(jax.random.uniform(third, (1, 1, 1, F), jnp.float32, math.log(0.3), math.log(3.0)))
    seg_scale = jnp.exp(jax.random.uniform(fourth, (SEGMENTS, 1, 1, 1), jnp.float32, 0.0, math.log(3.0)))
    top_bins = (lax.iota(jnp.int32, F) >= F - 8).astype(jnp.float32).reshape(1, 1, 1, F)
    narrow = jnp.clip(jax.random.normal(jax.random.fold_in(first, 7), (SEGMENTS, 1, 2, F), jnp.float32), -2.5, 2.5)
    narrow = 3.0 * narrow * top_bins
    base = jnp.clip(jax.random.normal(first, shape, jnp.float32), -6.0, 6.0)
    values = base * channel_scale * bin_scale * seg_scale + narrow * channel_scale * seg_scale
    return values.astype(jnp.bfloat16)


def place_ends(array, stream_key, low, top_value):
    longest = array.shape.index(max(array.shape))
    spots = []
    for shift in (0, 1):
        where = [jax.random.randint(jax.random.fold_in(stream_key, axis), (), 0, length) for axis, length in enumerate(array.shape)]
        where[longest] = (where[longest] + shift) % array.shape[longest]
        spots.append(tuple(where))
    return array.at[spots[0]].set(low).at[spots[1]].set(top_value)


def shared_out(key, own, number, rows, count, top, reach, slope):
    ranking = jax.random.permutation(key, count)
    crowded, ordinary = load_shares(count, rows * top, reach, slope, True), load_shares(count, rows * top, reach, slope, False)
    places = jnp.arange(count)

    def named(tallies, offset_by):
        used = int((tallies > 0).sum())
        fixed = max(1, used // 4)
        moved = fixed + (places - fixed + offset_by * (used - fixed)) % max(1, count - fixed)
        return jnp.zeros((count,), jnp.int32).at[ranking[jnp.where(places < fixed, places, moved)]].set(jnp.asarray(tallies, jnp.int32))

    tallies = jnp.where(number % 4 == 0, named(crowded, number // 4), named(ordinary, number - number // 4 - 1))
    mixed = jax.random.permutation(jax.random.fold_in(own, 3), count)
    source_of, sink = mixed[0:count // 2 * 2:2], mixed[1:count // 2 * 2:2]
    slack = jnp.minimum(tallies[source_of] - 1, reach - tallies[sink]) // 2
    slack = jnp.where((source_of == ranking[0]) | (sink == ranking[0]) | (tallies[sink] == 0), 0, jnp.maximum(slack, 0))
    moved = jax.random.randint(jax.random.fold_in(own, 4), (count // 2,), 0, 1 << 20) % (slack + 1)
    tallies = tallies.at[source_of].add(-moved).at[sink].add(moved)
    labels = jnp.searchsorted(jnp.cumsum(tallies), jnp.arange(rows * top), side="right").astype(jnp.int32)
    listing = labels.reshape(top, rows).T
    listing = listing[jax.random.permutation(jax.random.fold_in(own, 1), rows)]
    offset_by = jax.random.randint(jax.random.fold_in(own, 2), (rows, 1), 0, top)
    return jnp.take_along_axis(listing, (jnp.arange(top)[None, :] + offset_by) % top, axis=1)


def load_shares(number_of, total, reach, skew, full):
    weights = [(1 << 20) // math.isqrt(rank ** skew) + 1 for rank in range(1, number_of + 1)]
    largest = reach if full else min(reach, max(-(-total // number_of), total * weights[0] // sum(weights)))
    least = 1 if total - largest >= number_of - 1 else 0
    given, surplus = [largest] + [least] * (number_of - 1), total - largest - least * (number_of - 1)
    while surplus > 0:
        free = [i for i in range(1, number_of) if given[i] < largest] or [i for i in range(1, number_of) if given[i] < reach]
        pool, left = sum([weights[i] for i in free]), surplus
        for i in free:
            more = min(reach - given[i], max(1, left * weights[i] // pool), surplus)
            given[i] = given[i] + more
            surplus = surplus - more
    return np.array(given)


def setup_inputs(seed: int = 0) -> dict:
    splits = jax.random.split(jax.random.key(seed), 4)
    spectra = draw_spectra(jax.random.fold_in(splits[3], 71), 0)
    owner_device_keys = jax.random.split(jax.random.fold_in(splits[1], 1), ROWS // PAIRS)
    owner_device_turns = jax.random.permutation(jax.random.fold_in(splits[1], 3), ROWS // PAIRS)
    owner_device = jax.vmap(lambda own, number: shared_out(jax.random.fold_in(splits[1], 2), own, number, PAIRS, N_BLK, 1, CAP, 2))(owner_device_keys, owner_device_turns).reshape((ROWS, 1))
    stack_slot = place_ends(jax.random.randint(splits[2], (ROWS,), 0, STACKS_DEV), jax.random.fold_in(splits[2], 1), 0, STACKS_DEV - 1).astype(jnp.int32)
    return {"spectra": spectra, "owner_device": owner_device, "stack_slot": stack_slot}


def whiten(spectra):
    seg_count, chan_count, part_count, freq_count = spectra.shape
    values = spectra.astype(jnp.float32).reshape(seg_count, chan_count, part_count, freq_count // WBAND, WBAND)
    power_mean = lax.optimization_barrier(jnp.mean(values * values, axis=(2, 4), keepdims=True))
    scaled = values * lax.rsqrt(power_mean + 1e-06)
    return scaled.reshape(seg_count, chan_count, part_count, freq_count).astype(jnp.bfloat16)

def lag_table(first_bin, bin_count, lag_first, lag_count, factor):
    bin_numbers = first_bin + lax.iota(jnp.int32, bin_count) + 1
    lag_steps = lag_first + lax.iota(jnp.int32, lag_count) - LAGS // 2
    wrapped = jnp.mod(bin_numbers[:, None] * lag_steps[None, :], NFFT)
    phases = wrapped.astype(jnp.float32) * (2.0 * math.pi / NFFT)
    both = jnp.concatenate([jnp.cos(phases), -jnp.sin(phases)], axis=0) * factor
    return both.astype(jnp.bfloat16)

def half_stack(partner, own_block):
    chan_count = own_block.shape[1]
    bin_count = own_block.shape[3]
    real_part = lax.optimization_barrier(jnp.sum(partner[:, :, None, 0, :] * own_block[:, None, :, 0, :] + partner[:, :, None, 1, :] * own_block[:, None, :, 1, :], axis=0))
    imag_part = lax.optimization_barrier(jnp.sum(partner[:, :, None, 1, :] * own_block[:, None, :, 0, :] - partner[:, :, None, 0, :] * own_block[:, None, :, 1, :], axis=0))
    joined = jnp.concatenate([real_part.reshape(chan_count * chan_count, bin_count), imag_part.reshape(chan_count * chan_count, bin_count)], axis=1)
    return joined.astype(jnp.bfloat16)

def reference(spectra, owner_device, stack_slot):
    whitened = whiten(spectra)
    lag_full = lag_table(0, F, 0, LAGS, (2.0 * F * SEGMENTS) ** (-0.5))
    blocks = whitened.reshape(SEGMENTS, N_BLK, CB, 2, F)

    def device_tiles(device):
        own_block = lax.dynamic_index_in_dim(blocks, device, 1, keepdims=False).astype(jnp.float32)
        tile_list = []
        for step_index in range(ROUNDS):
            source_block = device - (step_index + 1)
            partner = lax.dynamic_index_in_dim(blocks, jnp.maximum(source_block, 0), 1, keepdims=False).astype(jnp.float32)
            partner = jnp.where(source_block >= 0, partner, jnp.zeros_like(partner))
            running = jnp.zeros((CB * CB, LAGS), jnp.float32)
            for seg_group in range(N_SEG):
                first_seg = seg_group * SEG_DEV
                stacked = half_stack(partner[first_seg:first_seg + SEG_DEV], own_block[first_seg:first_seg + SEG_DEV])
                running = running + jnp.dot(stacked, lag_full, preferred_element_type=jnp.float32)
            tile_list.append(running.astype(jnp.bfloat16))
        return jnp.stack(tile_list)
    all_tiles = lax.map(device_tiles, jnp.arange(N_BLK, dtype=jnp.int32))
    target = owner_device[:, 0] * STACKS_DEV + stack_slot
    summed = jax.ops.segment_sum(all_tiles.reshape(ROWS, LAGS).astype(jnp.float32), target, num_segments=STACKS)
    return summed.astype(jnp.bfloat16)
```

```python
import functools
import math

import jax
import jax.numpy as jnp
import numpy as np
from jax import lax
from jax.experimental import pallas as pl
from jax.experimental.pallas import tpu as pltpu
from jax.sharding import PartitionSpec as P

F = 2048
NFFT = 16384
LAGS = 512
HALF = LAGS // 2
WBAND = 128
STACKS_DEV = 128
CB = 64
SEGS = 8
PAIRS = CB * CB
CAP = 64
GROUP = 16
GROUPS = F // GROUP
WIDE = 128
VMEM = pl.BlockSpec(memory_space=pltpu.VMEM)
SMEM = pl.BlockSpec(memory_space=pltpu.SMEM)


def lag_rows(factor):
    bins = np.arange(1, F + 1)

    def phases(lags):
        wrapped = (np.asarray(lags)[:, None] * bins[None, :]) % NFFT
        return wrapped.astype(np.float32) * np.float32(2.0 * math.pi / NFFT)

    scale = np.float32(factor)
    last = np.zeros((16, F), np.float32)
    last[0] = np.cos(phases([HALF]))[0] * scale
    cos_rows = np.concatenate([np.cos(phases(np.arange(HALF))) * scale, last])
    sin_rows = np.sin(phases(np.concatenate([[HALF], np.arange(1, HALF)]))) * scale
    return cos_rows.astype(jnp.bfloat16), sin_rows.astype(jnp.bfloat16)


def whiten_kernel(x_ref, o_ref):
    lane = lax.broadcasted_iota(jnp.int32, (CB, WIDE), 1) // GROUP
    for band in range(F // WBAND):
        parts = []
        for part in range(2):
            first = part * F + band * WBAND
            parts.append([x_ref[s, :, first : first + WBAND].astype(jnp.float32) for s in range(4)])
        values = []
        scales = []
        for s in range(4):
            power = jnp.sum(parts[0][s] * parts[0][s] + parts[1][s] * parts[1][s], axis=1, keepdims=True)
            scales.append(lax.rsqrt(power * (1.0 / (2 * WBAND)) + 1e-06))
        for part in range(2):
            for s in range(4):
                values.append(parts[part][s] * scales[s])
        for step in (1, 2, 4):
            low = (lane // step) % 2 == 0
            swapped = list(values)
            for q in range(8):
                if q & step:
                    continue
                a, b = values[q], values[q + step]
                swapped[q] = jnp.where(low, a, pltpu.roll(b, GROUP * step, 1))
                swapped[q + step] = jnp.where(low, pltpu.roll(a, WIDE - GROUP * step, 1), b)
            values = swapped
        for g in range(8):
            first = (band * 8 + g) * WIDE
            o_ref[:, first : first + WIDE] = values[g].astype(jnp.bfloat16)


def whiten(spectra):
    return pl.pallas_call(
        whiten_kernel,
        out_shape=jax.ShapeDtypeStruct((CB, GROUPS * WIDE), jnp.bfloat16),
        in_specs=[VMEM],
        out_specs=VMEM,
        compiler_params=pltpu.CompilerParams(vmem_limit_bytes=40 * 2**20),
        cost_estimate=pl.CostEstimate(flops=20_000_000, bytes_accessed=2**22, transcendentals=4096),
        name="whiten",
    )(spectra.reshape(4, CB, 2 * F))


def tile_kernel(chans, sign_ref, p_ref, o_ref, cos_ref, sin_ref, keep_ref, send_ref, g_re, g_im):
    unroll = 4
    row = lax.broadcasted_iota(jnp.int32, (GROUP, WIDE), 0)
    lane = lax.broadcasted_iota(jnp.int32, (GROUP, WIDE), 1)
    mask = jnp.where(row == lane % GROUP, 1.0, 0.0).astype(jnp.bfloat16)
    wide_lane = lax.broadcasted_iota(jnp.int32, (CB, WIDE), 1)
    turn = jnp.where(wide_lane < WIDE // 2, -1.0, 1.0).astype(jnp.bfloat16)
    zero = jnp.zeros((CB, WIDE), jnp.bfloat16)

    def one(group):
        cols = pl.ds(pl.multiple_of(group * WIDE, WIDE), WIDE)
        own = o_ref[:, cols]
        turned = jnp.concatenate([own[:, WIDE // 2 :], own[:, : WIDE // 2]], axis=1) * turn
        right = jnp.concatenate(
            [
                jnp.concatenate([own, zero], 1),
                jnp.concatenate([zero, own], 1),
                jnp.concatenate([turned, zero], 1),
                jnp.concatenate([zero, turned], 1),
            ],
            0,
        )
        spread = jnp.broadcast_to(p_ref[:, cols][:, None, :], (chans, GROUP, WIDE)) * mask[None]
        spread = spread.reshape(chans // 2, 2, GROUP, WIDE)
        left = jnp.concatenate([spread[:, 0], spread[:, 1]], axis=2).reshape(chans * 8, 2 * WIDE)
        out = lax.dot_general(
            left, right, (((1,), (1,)), ((), ())), preferred_element_type=jnp.float32
        ).astype(jnp.bfloat16)
        rows = pl.ds(pl.multiple_of(group * GROUP, GROUP), GROUP)
        for i in range(chans // 2):
            g_re[rows, i * WIDE : (i + 1) * WIDE] = out[i * GROUP : (i + 1) * GROUP, :WIDE]
            g_im[rows, i * WIDE : (i + 1) * WIDE] = out[i * GROUP : (i + 1) * GROUP, WIDE:]

    def body(i, carry):
        for u in range(unroll):
            one(i * unroll + u)
        return carry

    lax.fori_loop(0, GROUPS // unroll, body, 0)
    sign = sign_ref[0]
    top = lax.broadcasted_iota(jnp.int32, (HALF, 256), 0) == 0
    for j in range(chans * CB // 256):
        cols = slice(j * 256, (j + 1) * 256)
        even = jnp.dot(cos_ref[...], g_re[:, cols], preferred_element_type=jnp.float32)
        odd = jnp.dot(sin_ref[...], g_im[:, cols], preferred_element_type=jnp.float32)
        low, last = even[:HALF], even[HALF : HALF + 1]
        behind = jnp.where(top, last, low) + odd
        ahead = jnp.where(top, low, low - odd)
        keep_ref[:, cols] = jnp.where(sign > 0, behind, ahead)
        send_ref[:, cols] = jnp.where(sign > 0, ahead, behind).astype(jnp.bfloat16)


def tile_halves(chans, sign, partner, own, cos_rows, sin_rows):
    pairs = chans * CB
    return pl.pallas_call(
        functools.partial(tile_kernel, chans),
        out_shape=(
            jax.ShapeDtypeStruct((HALF, pairs), jnp.float32),
            jax.ShapeDtypeStruct((HALF, pairs), jnp.bfloat16),
        ),
        in_specs=[SMEM, VMEM, VMEM, VMEM, VMEM],
        out_specs=(VMEM, VMEM),
        scratch_shapes=[pltpu.VMEM((F, pairs), jnp.bfloat16)] * 2,
        compiler_params=pltpu.CompilerParams(vmem_limit_bytes=56 * 2**20),
        cost_estimate=pl.CostEstimate(
            flops=25_000_000_000 * chans // CB, bytes_accessed=2**23, transcendentals=0
        ),
        name="tiles",
    )(sign, partner, own, cos_rows, sin_rows)


def place_kernel(chunks, dest_ref, *refs):
    keeps, gots = refs[:chunks], refs[chunks : 2 * chunks]
    out_ref, rows, spread = refs[2 * chunks :]
    pairs = PAIRS // chunks
    for chunk in range(chunks):
        for j in range(pairs // 256):
            cols = slice(j * 256, (j + 1) * 256)
            total = keeps[chunk][:, cols] + gots[chunk][:, cols].astype(jnp.float32)
            first = chunk * pairs + j * 256
            rows[first : first + 256, :] = total.T

    def clear(i, carry):
        spread[pl.ds(pl.multiple_of(i * 64, 64), 64), :] = jnp.zeros((64, HALF), jnp.float32)
        return carry

    lax.fori_loop(0, spread.shape[0] // 64, clear, 0)

    def move(i, carry):
        for u in range(16):
            p = i * 16 + u
            spread[pl.ds(dest_ref[p], 1), :] = rows[pl.ds(p, 1), :]
        return carry

    lax.fori_loop(0, PAIRS // 16, move, 0)

    def finish(i, carry):
        at = pl.ds(pl.multiple_of(i * 64, 64), 64)
        out_ref[at, :] = spread[at, :].astype(jnp.bfloat16)
        return carry

    lax.fori_loop(0, spread.shape[0] // 64, finish, 0)


def place_rows(dest, keeps, gots, rows_out):
    chunks = len(keeps)
    return pl.pallas_call(
        functools.partial(place_kernel, chunks),
        out_shape=jax.ShapeDtypeStruct((rows_out, HALF), jnp.bfloat16),
        in_specs=[SMEM] + [VMEM] * (2 * chunks),
        out_specs=VMEM,
        scratch_shapes=[
            pltpu.VMEM((PAIRS, HALF), jnp.float32),
            pltpu.VMEM((rows_out, HALF), jnp.float32),
        ],
        compiler_params=pltpu.CompilerParams(vmem_limit_bytes=56 * 2**20),
        name="place",
    )(dest, *keeps, *gots)


def local(spectra, owner_device, stack_slot):
    blk_devices = lax.axis_size("blk")
    seg = lax.axis_index("seg")
    factor = (2.0 * F * SEGS) ** (-0.5)
    cos_rows, sin_rows = lag_rows(factor)
    chunks = 2
    chans = CB // chunks
    whitened = whiten(spectra)
    ahead = [(b, b + 1) for b in range(blk_devices - 1)]
    partners = [
        lax.ppermute(whitened[i * chans : (i + 1) * chans], "blk", ahead) for i in range(chunks)
    ]
    sign = jnp.where(seg == 0, 1, -1).astype(jnp.int32).reshape(1)
    keeps, gots = [], []
    for partner in partners:
        keep, send = tile_halves(chans, sign, partner, whitened, cos_rows, sin_rows)
        keeps.append(keep)
        gots.append(lax.ppermute(send, "seg", [(0, 1), (1, 0)]))

    owner_rows = owner_device[:, 0]
    owner_hot = (owner_rows[:, None] == lax.iota(jnp.int32, blk_devices)[None, :]).astype(jnp.int32)
    position = jnp.sum((jnp.cumsum(owner_hot, axis=0) - owner_hot) * owner_hot, axis=1)
    destination = owner_rows * CAP + position
    outgoing = place_rows(destination, keeps, gots, blk_devices * CAP)
    outgoing_slot = (
        jnp.full((blk_devices * CAP, 1), -1, jnp.int32).at[destination, 0].set(stack_slot)
    )
    received = lax.all_to_all(outgoing, "blk", split_axis=0, concat_axis=0, tiled=True)
    received_slot = lax.all_to_all(outgoing_slot, "blk", split_axis=0, concat_axis=0, tiled=True)
    one_hot = (lax.iota(jnp.int32, STACKS_DEV)[:, None] == received_slot[:, 0][None, :]).astype(
        jnp.bfloat16
    )
    stacks = jnp.dot(one_hot, received, preferred_element_type=jnp.float32)
    lags = lax.iota(jnp.int32, HALF)
    turned = jnp.roll(stacks[:, ::-1], 1, axis=1)
    stacks = jnp.where(seg == 0, turned, stacks)
    return stacks.astype(jnp.bfloat16)


def solution(mesh):
    placed = (P("seg", "blk", None, None), P("blk", None), P("blk"))
    return jax.shard_map(
        local, mesh=mesh, in_specs=placed, out_specs=P("blk", "seg"), check_vma=False
    )
```

```python
import functools
import math

import jax
import jax.numpy as jnp
import numpy as np
from jax import lax
from jax.experimental import pallas as pl
from jax.experimental.pallas import tpu as pltpu
from jax.sharding import PartitionSpec as P

F = 2048
NFFT = 16384
LAGS = 512
HALF = LAGS // 2
WBAND = 128
STACKS_DEV = 128
CB = 64
SEGS = 8
PAIRS = CB * CB
CAP = 64
GROUP = 16
GROUPS = F // GROUP
WIDE = 128
VMEM = pl.BlockSpec(memory_space=pltpu.VMEM)
SMEM = pl.BlockSpec(memory_space=pltpu.SMEM)


def lag_rows(factor):
    bins = np.arange(1, F + 1)

    def phases(lags):
        wrapped = (np.asarray(lags)[:, None] * bins[None, :]) % NFFT
        return wrapped.astype(np.float32) * np.float32(2.0 * math.pi / NFFT)

    scale = np.float32(factor)
    last = np.zeros((16, F), np.float32)
    last[0] = np.cos(phases([HALF]))[0] * scale
    cos_rows = np.concatenate([np.cos(phases(np.arange(HALF))) * scale, last])
    sin_rows = np.sin(phases(np.concatenate([[HALF], np.arange(1, HALF)]))) * scale
    return cos_rows.astype(jnp.bfloat16), sin_rows.astype(jnp.bfloat16)


def whiten_kernel(x_ref, o_ref):
    lane = lax.broadcasted_iota(jnp.int32, (CB, WIDE), 1) // GROUP
    for band in range(F // WBAND):
        parts = []
        for part in range(2):
            first = part * F + band * WBAND
            parts.append([x_ref[s, :, first : first + WBAND].astype(jnp.float32) for s in range(4)])
        values = []
        scales = []
        for s in range(4):
            power = jnp.sum(parts[0][s] * parts[0][s] + parts[1][s] * parts[1][s], axis=1, keepdims=True)
            scales.append(lax.rsqrt(power * (1.0 / (2 * WBAND)) + 1e-06))
        for part in range(2):
            for s in range(4):
                values.append(parts[part][s] * scales[s])
        for step in (1, 2, 4):
            low = (lane // step) % 2 == 0
            swapped = list(values)
            for q in range(8):
                if q & step:
                    continue
                a, b = values[q], values[q + step]
                swapped[q] = jnp.where(low, a, pltpu.roll(b, GROUP * step, 1))
                swapped[q + step] = jnp.where(low, pltpu.roll(a, WIDE - GROUP * step, 1), b)
            values = swapped
        for g in range(8):
            first = (band * 8 + g) * WIDE
            o_ref[:, first : first + WIDE] = values[g].astype(jnp.bfloat16)


def whiten(spectra):
    return pl.pallas_call(
        whiten_kernel,
        out_shape=jax.ShapeDtypeStruct((CB, GROUPS * WIDE), jnp.bfloat16),
        in_specs=[VMEM],
        out_specs=VMEM,
        compiler_params=pltpu.CompilerParams(vmem_limit_bytes=40 * 2**20),
        cost_estimate=pl.CostEstimate(flops=20_000_000, bytes_accessed=2**22, transcendentals=4096),
        name="whiten",
    )(spectra.reshape(4, CB, 2 * F))


def tile_kernel(chans, sign_ref, p_ref, o_ref, cos_ref, sin_ref, keep_ref, send_ref, g_re, g_im):
    unroll = 4
    row = lax.broadcasted_iota(jnp.int32, (GROUP, WIDE), 0)
    lane = lax.broadcasted_iota(jnp.int32, (GROUP, WIDE), 1)
    mask = jnp.where(row == lane % GROUP, 1.0, 0.0).astype(jnp.bfloat16)
    wide_lane = lax.broadcasted_iota(jnp.int32, (CB, WIDE), 1)
    turn = jnp.where(wide_lane < WIDE // 2, -1.0, 1.0).astype(jnp.bfloat16)
    zero = jnp.zeros((CB, WIDE), jnp.bfloat16)

    def one(group):
        cols = pl.ds(pl.multiple_of(group * WIDE, WIDE), WIDE)
        own = o_ref[:, cols]
        turned = jnp.concatenate([own[:, WIDE // 2 :], own[:, : WIDE // 2]], axis=1) * turn
        right = jnp.concatenate(
            [
                jnp.concatenate([own, zero], 1),
                jnp.concatenate([zero, own], 1),
                jnp.concatenate([turned, zero], 1),
                jnp.concatenate([zero, turned], 1),
            ],
            0,
        )
        spread = jnp.broadcast_to(p_ref[:, cols][:, None, :], (chans, GROUP, WIDE)) * mask[None]
        spread = spread.reshape(chans // 2, 2, GROUP, WIDE)
        left = jnp.concatenate([spread[:, 0], spread[:, 1]], axis=2).reshape(chans * 8, 2 * WIDE)
        out = lax.dot_general(
            left, right, (((1,), (1,)), ((), ())), preferred_element_type=jnp.float32
        ).astype(jnp.bfloat16)
        rows = pl.ds(pl.multiple_of(group * GROUP, GROUP), GROUP)
        for i in range(chans // 2):
            g_re[rows, i * WIDE : (i + 1) * WIDE] = out[i * GROUP : (i + 1) * GROUP, :WIDE]
            g_im[rows, i * WIDE : (i + 1) * WIDE] = out[i * GROUP : (i + 1) * GROUP, WIDE:]

    def body(i, carry):
        for u in range(unroll):
            one(i * unroll + u)
        return carry

    lax.fori_loop(0, GROUPS // unroll, body, 0)
    sign = sign_ref[0]
    top = lax.broadcasted_iota(jnp.int32, (HALF, 256), 0) == 0
    for j in range(chans * CB // 256):
        cols = slice(j * 256, (j + 1) * 256)
        even = jnp.dot(cos_ref[...], g_re[:, cols], preferred_element_type=jnp.float32)
        odd = jnp.dot(sin_ref[...], g_im[:, cols], preferred_element_type=jnp.float32)
        low, last = even[:HALF], even[HALF : HALF + 1]
        behind = jnp.where(top, last, low) + odd
        ahead = jnp.where(top, low, low - odd)
        keep_ref[:, cols] = jnp.where(sign > 0, behind, ahead)
        send_ref[:, cols] = jnp.where(sign > 0, ahead, behind).astype(jnp.bfloat16)


def tile_halves(chans, sign, partner, own, cos_rows, sin_rows):
    pairs = chans * CB
    return pl.pallas_call(
        functools.partial(tile_kernel, chans),
        out_shape=(
            jax.ShapeDtypeStruct((HALF, pairs), jnp.float32),
            jax.ShapeDtypeStruct((HALF, pairs), jnp.bfloat16),
        ),
        in_specs=[SMEM, VMEM, VMEM, VMEM, VMEM],
        out_specs=(VMEM, VMEM),
        scratch_shapes=[pltpu.VMEM((F, pairs), jnp.bfloat16)] * 2,
        compiler_params=pltpu.CompilerParams(vmem_limit_bytes=56 * 2**20),
        cost_estimate=pl.CostEstimate(
            flops=25_000_000_000 * chans // CB, bytes_accessed=2**23, transcendentals=0
        ),
        name="tiles",
    )(sign, partner, own, cos_rows, sin_rows)


def place_kernel(chunks, dest_ref, *refs):
    keeps, gots = refs[:chunks], refs[chunks : 2 * chunks]
    out_ref, rows, spread = refs[2 * chunks :]
    pairs = PAIRS // chunks
    for chunk in range(chunks):
        for j in range(pairs // 256):
            cols = slice(j * 256, (j + 1) * 256)
            total = keeps[chunk][:, cols] + gots[chunk][:, cols].astype(jnp.float32)
            first = chunk * pairs + j * 256
            rows[first : first + 256, :] = total.T

    def clear(i, carry):
        spread[pl.ds(pl.multiple_of(i * 64, 64), 64), :] = jnp.zeros((64, HALF), jnp.float32)
        return carry

    lax.fori_loop(0, spread.shape[0] // 64, clear, 0)

    def move(i, carry):
        for u in range(16):
            p = i * 16 + u
            spread[pl.ds(dest_ref[p], 1), :] = rows[pl.ds(p, 1), :]
        return carry

    lax.fori_loop(0, PAIRS // 16, move, 0)

    def finish(i, carry):
        at = pl.ds(pl.multiple_of(i * 64, 64), 64)
        out_ref[at, :] = spread[at, :].astype(jnp.bfloat16)
        return carry

    lax.fori_loop(0, spread.shape[0] // 64, finish, 0)


def place_rows(dest, keeps, gots, rows_out):
    chunks = len(keeps)
    return pl.pallas_call(
        functools.partial(place_kernel, chunks),
        out_shape=jax.ShapeDtypeStruct((rows_out, HALF), jnp.bfloat16),
        in_specs=[SMEM] + [VMEM] * (2 * chunks),
        out_specs=VMEM,
        scratch_shapes=[
            pltpu.VMEM((PAIRS, HALF), jnp.float32),
            pltpu.VMEM((rows_out, HALF), jnp.float32),
        ],
        compiler_params=pltpu.CompilerParams(vmem_limit_bytes=56 * 2**20),
        name="place",
    )(dest, *keeps, *gots)


SLOTS_A, SLOTS_C, SLOTS_B = 48, 48, 32
AC = SLOTS_A + SLOTS_C


def place_of(z, x, y, core):
    return ((z * 2 + x) * 4 + y) * 2 + core


def reduce_kernel(
    rows_ref, slots_ref, out_ref,
    sib_rows, sib_slots, da, db, dc, ra, rb, rc, sa, sb, sc, ra2, rb2, rc2, t, tb, rt, rtb,
    send_sem, recv_sem,
):
    blk = lax.axis_index("blk")
    seg = lax.axis_index("seg")
    core = blk % 2
    y = (blk // 2) % 4
    x = (blk // 8) % 2
    z = blk // 16
    other = (place_of(z, x, y, 1 - core), seg)
    across = (place_of(z, 1 - x, y, core), seg)

    def along_y(k):
        return (place_of(z, x, (y + k) % 4, core), seg)

    def along_z(k):
        return (place_of((z + k) % 8, x, y, core), seg)

    partners = [other, across] + [along_y(k) for k in (1, 2, 3)] + [along_z(k) for k in range(1, 8)]
    barrier = pltpu.get_barrier_semaphore()
    for partner in partners:
        pl.semaphore_signal(barrier, inc=1, device_id=partner, device_id_type=pl.DeviceIdType.MESH)
    pl.semaphore_wait(barrier, len(partners))
    used = [0]

    def copy(src, dst, device):
        i = used[0]
        used[0] += 1
        made = pltpu.make_async_remote_copy(
            src_ref=src, dst_ref=dst, send_sem=send_sem.at[i], recv_sem=recv_sem.at[i],
            device_id=device, device_id_type=pl.DeviceIdType.MESH,
        )
        made.start()
        return made

    half = CB * CAP
    copies = [
        copy(rows_ref.at[pl.ds((1 - core) * half, half)], sib_rows, other),
        copy(slots_ref.at[pl.ds((1 - core) * CB, CB)], sib_slots, other),
    ]
    for made in copies:
        made.wait()
    lane = lax.broadcasted_iota(jnp.int32, (1, STACKS_DEV), 1)
    slot = lax.broadcasted_iota(jnp.int32, (STACKS_DEV, STACKS_DEV), 0)

    def dense(i, carry):
        zz, xx, yy = i // 8, (i // 4) % 2, i % 4
        names = jnp.where(
            lane < CAP, slots_ref[pl.ds(core * CB + i, 1), :], sib_slots[pl.ds(i, 1), :]
        )
        hot = jnp.where(slot == names, 1.0, 0.0).astype(jnp.bfloat16)
        mine = rows_ref[pl.ds(pl.multiple_of(core * half + i * CAP, CAP), CAP), :]
        theirs = sib_rows[pl.ds(pl.multiple_of(i * CAP, CAP), CAP), :]
        total = jnp.dot(
            hot, jnp.concatenate([mine, theirs], 0), preferred_element_type=jnp.float32
        ).astype(jnp.bfloat16)
        da[yy, zz * 2 + xx] = total[:SLOTS_A]
        dc[xx, zz * 4 + yy] = total[SLOTS_A:AC]
        db[zz, xx * 4 + yy] = total[AC:]
        return carry

    lax.fori_loop(0, CB, dense, 0)
    first_c = [copy(dc.at[1 - x], rc, across)]
    first_a = [copy(da.at[(y + k) % 4], ra.at[k - 1], along_y(k)) for k in (1, 2, 3)]
    first_b = [copy(db.at[(z + k) % 8], rb.at[k - 1], along_z(k)) for k in range(1, 8)]
    copies = first_c + first_a + first_b

    def wide(value):
        return value.astype(jnp.float32)

    for made in first_c:
        made.wait()

    def sum_c(i, carry):
        total = wide(dc[x, i]) + wide(rc[i])
        sc[i % 4, i // 4] = total.astype(jnp.bfloat16)
        return carry

    lax.fori_loop(0, 32, sum_c, 0)
    second_c = [copy(sc.at[(y + k) % 4], rc2.at[k - 1], along_y(k)) for k in (1, 2, 3)]
    for made in first_a:
        made.wait()

    def sum_a(i, carry):
        total = wide(da[y, i])
        for k in range(3):
            total += wide(ra[k, i])
        sa[i % 2, i // 2] = total.astype(jnp.bfloat16)
        return carry

    lax.fori_loop(0, 16, sum_a, 0)
    second_a = [copy(sa.at[1 - x], ra2, across)]
    for made in first_b:
        made.wait()

    def sum_b(i, carry):
        total = wide(db[z, i])
        for k in range(7):
            total += wide(rb[k, i])
        sb[i % 4, i // 4] = total.astype(jnp.bfloat16)
        return carry

    lax.fori_loop(0, 8, sum_b, 0)
    second_b = [copy(sb.at[(y + k) % 4], rb2.at[k - 1], along_y(k)) for k in (1, 2, 3)]
    for made in second_a + second_c:
        made.wait()

    def sum_ac(i, carry):
        t[i, :SLOTS_A] = (wide(sa[x, i]) + wide(ra2[i])).astype(jnp.bfloat16)
        total = wide(sc[y, i])
        for k in range(3):
            total += wide(rc2[k, i])
        t[i, SLOTS_A:] = total.astype(jnp.bfloat16)
        return carry

    lax.fori_loop(0, 8, sum_ac, 0)
    third = [copy(t.at[(z + k) % 8], rt.at[k - 1], along_z(k)) for k in range(1, 8)]
    for made in second_b:
        made.wait()

    def sum_b2(i, carry):
        total = wide(sb[y, i])
        for k in range(3):
            total += wide(rb2[k, i])
        tb[i] = total.astype(jnp.bfloat16)
        return carry

    lax.fori_loop(0, 2, sum_b2, 0)
    third_b = [copy(tb.at[1 - x], rtb, across)]
    for made in third + third_b:
        made.wait()
    total = wide(t[z])
    for k in range(7):
        total += wide(rt[k])
    out_ref[:AC, :] = total
    out_ref[AC:, :] = wide(tb[x]) + wide(rtb[...])


def reduce_rows(rows, slots):
    def buf(*shape):
        return pltpu.VMEM((*shape, HALF), jnp.bfloat16)

    a, b, c = SLOTS_A, SLOTS_B, SLOTS_C
    count = 2 + 1 + 3 + 7 + 3 + 1 + 3 + 7 + 1
    return pl.pallas_call(
        reduce_kernel,
        out_shape=jax.ShapeDtypeStruct((STACKS_DEV, HALF), jnp.float32),
        in_specs=[VMEM, VMEM],
        out_specs=VMEM,
        scratch_shapes=[
            buf(CB * CAP), pltpu.VMEM((CB, STACKS_DEV), jnp.int32),
            buf(4, 16, a), buf(8, 8, b), buf(2, 32, c), buf(3, 16, a), buf(7, 8, b), buf(32, c),
            buf(2, 8, a), buf(4, 2, b), buf(4, 8, c), buf(8, a), buf(3, 2, b), buf(3, 8, c),
            buf(8, AC), buf(2, b), buf(7, AC), buf(b),
            pltpu.SemaphoreType.DMA((count,)), pltpu.SemaphoreType.DMA((count,)),
        ],
        compiler_params=pltpu.CompilerParams(
            collective_id=1, has_side_effects=True, vmem_limit_bytes=40 * 2**20
        ),
        cost_estimate=pl.CostEstimate(flops=2_000_000_000, bytes_accessed=2**23, transcendentals=0),
        name="reduce_rows",
    )(rows, slots)


def local(spectra, owner_device, stack_slot):
    blk_devices = lax.axis_size("blk")
    seg = lax.axis_index("seg")
    factor = (2.0 * F * SEGS) ** (-0.5)
    cos_rows, sin_rows = lag_rows(factor)
    chunks = 2
    chans = CB // chunks
    whitened = whiten(spectra)
    ahead = [(b, b + 1) for b in range(blk_devices - 1)]
    partners = [
        lax.ppermute(whitened[i * chans : (i + 1) * chans], "blk", ahead) for i in range(chunks)
    ]
    sign = jnp.where(seg == 0, 1, -1).astype(jnp.int32).reshape(1)
    keeps, gots = [], []
    for partner in partners:
        keep, send = tile_halves(chans, sign, partner, whitened, cos_rows, sin_rows)
        keeps.append(keep)
        gots.append(lax.ppermute(send, "seg", [(0, 1), (1, 0)]))

    owner_rows = owner_device[:, 0]
    ordered = (owner_rows % 2) * CB + owner_rows // 2
    hot = ordered[:, None] == lax.iota(jnp.int32, blk_devices)[None, :]
    count = hot.astype(jnp.int32)
    position = jnp.sum((jnp.cumsum(count, axis=0) - count) * count, axis=1)
    place_hot = position[:, None] == lax.iota(jnp.int32, STACKS_DEV)[None, :] % CAP
    named = jnp.where(place_hot, (stack_slot + 1)[:, None], 0).astype(jnp.bfloat16)
    slots = lax.dot_general(
        hot.astype(jnp.bfloat16), named, (((0,), (0,)), ((), ())), preferred_element_type=jnp.float32
    )
    slots = slots.astype(jnp.int32) - 1
    outgoing = place_rows(ordered * CAP + position, keeps, gots, blk_devices * CAP)
    stacks = reduce_rows(outgoing, slots)
    lags = lax.iota(jnp.int32, HALF)
    turned = jnp.roll(stacks[:, ::-1], 1, axis=1)
    stacks = jnp.where(seg == 0, turned, stacks)
    return stacks.astype(jnp.bfloat16)


def solution(mesh):
    placed = (P("seg", "blk", None, None), P("blk", None), P("blk"))
    return jax.shard_map(
        local, mesh=mesh, in_specs=placed, out_specs=P("blk", "seg"), check_vma=False
    )
```

```python
import functools
import math

import jax
import jax.numpy as jnp
import numpy as np
from jax import lax
from jax.experimental import pallas as pl
from jax.experimental.pallas import tpu as pltpu
from jax.sharding import PartitionSpec as P

F = 2048
NFFT = 16384
LAGS = 512
HALF = LAGS // 2
WBAND = 128
STACKS_DEV = 128
CB = 64
SEGS = 8
PAIRS = CB * CB
CAP = 64
GROUP = 16
GROUPS = F // GROUP
WIDE = 128
VMEM = pl.BlockSpec(memory_space=pltpu.VMEM)
SMEM = pl.BlockSpec(memory_space=pltpu.SMEM)


def lag_rows(factor):
    bins = np.arange(1, F + 1)

    def phases(lags):
        wrapped = (np.asarray(lags)[:, None] * bins[None, :]) % NFFT
        return wrapped.astype(np.float32) * np.float32(2.0 * math.pi / NFFT)

    scale = np.float32(factor)
    last = np.zeros((16, F), np.float32)
    last[0] = np.cos(phases([HALF]))[0] * scale
    cos_rows = np.concatenate([np.cos(phases(np.arange(HALF))) * scale, last])
    sin_rows = np.sin(phases(np.concatenate([[HALF], np.arange(1, HALF)]))) * scale
    return cos_rows.astype(jnp.bfloat16), sin_rows.astype(jnp.bfloat16)


def whiten_kernel(x_ref, o_ref):
    lane = lax.broadcasted_iota(jnp.int32, (CB, WIDE), 1) // GROUP
    for band in range(F // WBAND):
        parts = []
        for part in range(2):
            first = part * F + band * WBAND
            parts.append([x_ref[s, :, first : first + WBAND].astype(jnp.float32) for s in range(4)])
        values = []
        scales = []
        for s in range(4):
            power = jnp.sum(parts[0][s] * parts[0][s] + parts[1][s] * parts[1][s], axis=1, keepdims=True)
            scales.append(lax.rsqrt(power * (1.0 / (2 * WBAND)) + 1e-06))
        for part in range(2):
            for s in range(4):
                values.append(parts[part][s] * scales[s])
        for step in (1, 2, 4):
            low = (lane // step) % 2 == 0
            swapped = list(values)
            for q in range(8):
                if q & step:
                    continue
                a, b = values[q], values[q + step]
                swapped[q] = jnp.where(low, a, pltpu.roll(b, GROUP * step, 1))
                swapped[q + step] = jnp.where(low, pltpu.roll(a, WIDE - GROUP * step, 1), b)
            values = swapped
        for g in range(8):
            first = (band * 8 + g) * WIDE
            o_ref[:, first : first + WIDE] = values[g].astype(jnp.bfloat16)


def whiten(spectra):
    return pl.pallas_call(
        whiten_kernel,
        out_shape=jax.ShapeDtypeStruct((CB, GROUPS * WIDE), jnp.bfloat16),
        in_specs=[VMEM],
        out_specs=VMEM,
        compiler_params=pltpu.CompilerParams(vmem_limit_bytes=40 * 2**20),
        cost_estimate=pl.CostEstimate(flops=20_000_000, bytes_accessed=2**22, transcendentals=4096),
        name="whiten",
    )(spectra.reshape(4, CB, 2 * F))


def tile_kernel(chans, sign_ref, p_ref, o_ref, cos_ref, sin_ref, keep_ref, send_ref, g_re, g_im):
    unroll = 32
    row = lax.broadcasted_iota(jnp.int32, (GROUP, WIDE), 0)
    lane = lax.broadcasted_iota(jnp.int32, (GROUP, WIDE), 1)
    mask = jnp.where(row == lane % GROUP, 1.0, 0.0).astype(jnp.bfloat16)
    wide_lane = lax.broadcasted_iota(jnp.int32, (CB, WIDE), 1)
    turn = jnp.where(wide_lane < WIDE // 2, -1.0, 1.0).astype(jnp.bfloat16)

    def one(group):
        cols = pl.ds(pl.multiple_of(group * WIDE, WIDE), WIDE)
        own = o_ref[:, cols]
        turned = jnp.concatenate([own[:, CB:], own[:, :CB]], axis=1) * turn
        spread = jnp.broadcast_to(p_ref[:, cols][:, None, :], (chans, GROUP, WIDE)) * mask[None]
        out = lax.dot_general(
            spread.reshape(chans * GROUP, WIDE),
            jnp.concatenate([own, turned], 0),
            (((1,), (1,)), ((), ())),
            preferred_element_type=jnp.float32,
        ).astype(jnp.bfloat16)
        rows = pl.ds(pl.multiple_of(group * GROUP, GROUP), GROUP)
        for i in range(chans // 2):
            first = out[2 * i * GROUP : (2 * i + 1) * GROUP]
            second = out[(2 * i + 1) * GROUP : (2 * i + 2) * GROUP]
            pair = slice(i * WIDE, (i + 1) * WIDE)
            g_re[rows, pair] = jnp.concatenate([first[:, :CB], second[:, :CB]], 1)
            g_im[rows, pair] = jnp.concatenate([first[:, CB:], second[:, CB:]], 1)

    def body(i, carry):
        for u in range(unroll):
            one(i * unroll + u)
        return carry

    lax.fori_loop(0, GROUPS // unroll, body, 0)
    sign = sign_ref[0]
    top = lax.broadcasted_iota(jnp.int32, (HALF, 256), 0) == 0
    for j in range(chans * CB // 256):
        cols = slice(j * 256, (j + 1) * 256)
        even = jnp.dot(cos_ref[...], g_re[:, cols], preferred_element_type=jnp.float32)
        odd = jnp.dot(sin_ref[...], g_im[:, cols], preferred_element_type=jnp.float32)
        low, last = even[:HALF], even[HALF : HALF + 1]
        behind = jnp.where(top, last, low) + odd
        ahead = jnp.where(top, low, low - odd)
        keep_ref[:, cols] = jnp.where(sign > 0, behind, ahead)
        send_ref[:, cols] = jnp.where(sign > 0, ahead, behind).astype(jnp.bfloat16)


def tile_halves(chans, sign, partner, own, cos_rows, sin_rows):
    pairs = chans * CB
    return pl.pallas_call(
        functools.partial(tile_kernel, chans),
        out_shape=(
            jax.ShapeDtypeStruct((HALF, pairs), jnp.float32),
            jax.ShapeDtypeStruct((HALF, pairs), jnp.bfloat16),
        ),
        in_specs=[SMEM, VMEM, VMEM, VMEM, VMEM],
        out_specs=(VMEM, VMEM),
        scratch_shapes=[pltpu.VMEM((F, pairs), jnp.bfloat16)] * 2,
        compiler_params=pltpu.CompilerParams(vmem_limit_bytes=24 * 2**20),
        cost_estimate=pl.CostEstimate(
            flops=25_000_000_000 * chans // CB, bytes_accessed=2**23, transcendentals=0
        ),
        name="tiles",
    )(sign, partner, own, cos_rows, sin_rows)


def place_kernel(chunks, dest_ref, *refs):
    keeps, gots = refs[:chunks], refs[chunks : 2 * chunks]
    out_ref, rows, spread = refs[2 * chunks :]
    pairs = PAIRS // chunks
    for chunk in range(chunks):
        for j in range(pairs // 256):
            cols = slice(j * 256, (j + 1) * 256)
            total = keeps[chunk][:, cols] + gots[chunk][:, cols].astype(jnp.float32)
            turned = total.T
            for side in range(2):
                at = pl.ds((chunk * pairs + j * 256) * 2 + side, 256, stride=2)
                rows[at, :] = turned[:, side * WIDE : (side + 1) * WIDE]

    def clear(i, carry):
        spread[pl.ds(pl.multiple_of(i * 512, 512), 512), :] = jnp.zeros((512, WIDE), jnp.float32)
        return carry

    lax.fori_loop(0, spread.shape[0] // 512, clear, 0)

    def move(i, carry):
        for u in range(64):
            p = i * 64 + u
            to = pl.multiple_of(dest_ref[p] * 2, 2)
            spread[pl.ds(to, 2), :] = rows[pl.ds(pl.multiple_of(p * 2, 2), 2), :]
        return carry

    lax.fori_loop(0, PAIRS // 64, move, 0)

    def finish(i, carry):
        at = pl.ds(pl.multiple_of(i * 512, 512), 512)
        out_ref[at, :] = spread[at, :].astype(jnp.bfloat16)
        return carry

    lax.fori_loop(0, spread.shape[0] // 512, finish, 0)


def place_rows(dest, keeps, gots, rows_out):
    chunks = len(keeps)
    return pl.pallas_call(
        functools.partial(place_kernel, chunks),
        out_shape=jax.ShapeDtypeStruct((2 * rows_out, WIDE), jnp.bfloat16),
        in_specs=[SMEM] + [VMEM] * (2 * chunks),
        out_specs=VMEM,
        scratch_shapes=[
            pltpu.VMEM((2 * PAIRS, WIDE), jnp.float32),
            pltpu.VMEM((2 * rows_out, WIDE), jnp.float32),
        ],
        compiler_params=pltpu.CompilerParams(vmem_limit_bytes=28 * 2**20),
        name="place",
    )(dest, *keeps, *gots)


SLOTS_A, SLOTS_C, SLOTS_B = 48, 48, 32
AC = SLOTS_A + SLOTS_C


def place_of(z, x, y, core):
    return ((z * 2 + x) * 4 + y) * 2 + core


def reduce_kernel(
    rows_ref, slots_ref, out_ref,
    sib_rows, sib_slots, da, db, dc, ra, rb, rc, sa, sb, sc, ra2, rb2, rc2, t, tb, rt, rtb,
    send_sem, recv_sem,
):
    blk = lax.axis_index("blk")
    seg = lax.axis_index("seg")
    core = blk % 2
    y = (blk // 2) % 4
    x = (blk // 8) % 2
    z = blk // 16
    other = (place_of(z, x, y, 1 - core), seg)
    across = (place_of(z, 1 - x, y, core), seg)

    def along_y(k):
        return (place_of(z, x, (y + k) % 4, core), seg)

    def along_z(k):
        return (place_of((z + k) % 8, x, y, core), seg)

    partners = [other, across] + [along_y(k) for k in (1, 2, 3)] + [along_z(k) for k in range(1, 8)]
    barrier = pltpu.get_barrier_semaphore()
    for partner in partners:
        pl.semaphore_signal(barrier, inc=1, device_id=partner, device_id_type=pl.DeviceIdType.MESH)
    pl.semaphore_wait(barrier, len(partners))
    used = [0]

    def copy(src, dst, device):
        i = used[0]
        used[0] += 1
        made = pltpu.make_async_remote_copy(
            src_ref=src, dst_ref=dst, send_sem=send_sem.at[i], recv_sem=recv_sem.at[i],
            device_id=device, device_id_type=pl.DeviceIdType.MESH,
        )
        made.start()
        return made

    half = 2 * CB * CAP
    copies = [
        copy(rows_ref.at[pl.ds((1 - core) * half, half)], sib_rows, other),
        copy(slots_ref.at[pl.ds((1 - core) * CB, CB)], sib_slots, other),
    ]
    for made in copies:
        made.wait()
    lane = lax.broadcasted_iota(jnp.int32, (1, 4 * CAP), 1)
    slot = lax.broadcasted_iota(jnp.int32, (STACKS_DEV, 4 * CAP), 0)
    span = 2 * CAP

    def dense_one(i):
        zz, xx, yy = i // 8, (i // 4) % 2, i % 4
        names = jnp.concatenate([slots_ref[pl.ds(core * CB + i, 1), :], sib_slots[pl.ds(i, 1), :]], 1)
        left = jnp.where(lane % 2 == 0, names, -1)
        right = jnp.where(lane % 2 == 1, names, -1)
        hot = jnp.concatenate([slot == left, slot == right], 0)
        mine = rows_ref[pl.ds(pl.multiple_of(core * half + i * span, span), span), :]
        theirs = sib_rows[pl.ds(pl.multiple_of(i * span, span), span), :]
        total = jnp.dot(
            jnp.where(hot, 1.0, 0.0).astype(jnp.bfloat16),
            jnp.concatenate([mine, theirs], 0),
            preferred_element_type=jnp.float32,
        ).astype(jnp.bfloat16)
        total = jnp.concatenate([total[:STACKS_DEV], total[STACKS_DEV:]], 1)
        da[yy, zz * 2 + xx] = total[:SLOTS_A]
        dc[xx, zz * 4 + yy] = total[SLOTS_A:AC]
        db[zz, xx * 4 + yy] = total[AC:]

    def dense(i, carry):
        for u in range(8):
            dense_one(i * 8 + u)
        return carry

    lax.fori_loop(0, CB // 8, dense, 0)
    first_c = [copy(dc.at[1 - x], rc, across)]
    first_a = [copy(da.at[(y + k) % 4], ra.at[k - 1], along_y(k)) for k in (1, 2, 3)]
    first_b = [copy(db.at[(z + k) % 8], rb.at[k - 1], along_z(k)) for k in range(1, 8)]
    copies = first_c + first_a + first_b

    def wide(value):
        return value.astype(jnp.float32)

    for made in first_c:
        made.wait()

    def sum_c(i, carry):
        total = wide(dc[x, i]) + wide(rc[i])
        sc[i % 4, i // 4] = total.astype(jnp.bfloat16)
        return carry

    lax.fori_loop(0, 32, sum_c, 0)
    second_c = [copy(sc.at[(y + k) % 4], rc2.at[k - 1], along_y(k)) for k in (1, 2, 3)]
    for made in first_a:
        made.wait()

    def sum_a(i, carry):
        total = wide(da[y, i])
        for k in range(3):
            total += wide(ra[k, i])
        sa[i % 2, i // 2] = total.astype(jnp.bfloat16)
        return carry

    lax.fori_loop(0, 16, sum_a, 0)
    second_a = [copy(sa.at[1 - x], ra2, across)]
    for made in first_b:
        made.wait()

    def sum_b(i, carry):
        total = wide(db[z, i])
        for k in range(7):
            total += wide(rb[k, i])
        sb[i % 4, i // 4] = total.astype(jnp.bfloat16)
        return carry

    lax.fori_loop(0, 8, sum_b, 0)
    second_b = [copy(sb.at[(y + k) % 4], rb2.at[k - 1], along_y(k)) for k in (1, 2, 3)]
    for made in second_a + second_c:
        made.wait()

    def sum_ac(i, carry):
        t[i, :SLOTS_A] = (wide(sa[x, i]) + wide(ra2[i])).astype(jnp.bfloat16)
        total = wide(sc[y, i])
        for k in range(3):
            total += wide(rc2[k, i])
        t[i, SLOTS_A:] = total.astype(jnp.bfloat16)
        return carry

    lax.fori_loop(0, 8, sum_ac, 0)
    third = [copy(t.at[(z + k) % 8], rt.at[k - 1], along_z(k)) for k in range(1, 8)]
    for made in second_b:
        made.wait()

    def sum_b2(i, carry):
        total = wide(sb[y, i])
        for k in range(3):
            total += wide(rb2[k, i])
        tb[i] = total.astype(jnp.bfloat16)
        return carry

    lax.fori_loop(0, 2, sum_b2, 0)
    third_b = [copy(tb.at[1 - x], rtb, across)]
    for made in third + third_b:
        made.wait()
    total = wide(t[z])
    for k in range(7):
        total += wide(rt[k])
    out_ref[:AC, :] = total
    out_ref[AC:, :] = wide(tb[x]) + wide(rtb[...])


def reduce_rows(rows, slots):
    def buf(*shape):
        return pltpu.VMEM((*shape, HALF), jnp.bfloat16)

    a, b, c = SLOTS_A, SLOTS_B, SLOTS_C
    count = 2 + 1 + 3 + 7 + 3 + 1 + 3 + 7 + 1
    return pl.pallas_call(
        reduce_kernel,
        out_shape=jax.ShapeDtypeStruct((STACKS_DEV, HALF), jnp.float32),
        in_specs=[VMEM, VMEM],
        out_specs=VMEM,
        scratch_shapes=[
            pltpu.VMEM((2 * CB * CAP, WIDE), jnp.bfloat16), pltpu.VMEM((CB, STACKS_DEV), jnp.int32),
            buf(4, 16, a), buf(8, 8, b), buf(2, 32, c), buf(3, 16, a), buf(7, 8, b), buf(32, c),
            buf(2, 8, a), buf(4, 2, b), buf(4, 8, c), buf(8, a), buf(3, 2, b), buf(3, 8, c),
            buf(8, AC), buf(2, b), buf(7, AC), buf(b),
            pltpu.SemaphoreType.DMA((count,)), pltpu.SemaphoreType.DMA((count,)),
        ],
        compiler_params=pltpu.CompilerParams(
            collective_id=1, has_side_effects=True, vmem_limit_bytes=40 * 2**20
        ),
        cost_estimate=pl.CostEstimate(flops=2_000_000_000, bytes_accessed=2**23, transcendentals=0),
        name="reduce_rows",
    )(rows, slots)


def local(spectra, owner_device, stack_slot):
    blk_devices = lax.axis_size("blk")
    seg = lax.axis_index("seg")
    factor = (2.0 * F * SEGS) ** (-0.5)
    cos_rows, sin_rows = lag_rows(factor)
    chunks = 4
    chans = CB // chunks
    whitened = whiten(spectra)
    ahead = [(b, b + 1) for b in range(blk_devices - 1)]
    partners = [
        lax.ppermute(whitened[i * chans : (i + 1) * chans], "blk", ahead) for i in range(chunks)
    ]
    sign = jnp.where(seg == 0, 1, -1).astype(jnp.int32).reshape(1)
    keeps, gots = [], []
    for partner in partners:
        keep, send = tile_halves(chans, sign, partner, whitened, cos_rows, sin_rows)
        keeps.append(keep)
        gots.append(lax.ppermute(send, "seg", [(0, 1), (1, 0)]))

    owner_rows = owner_device[:, 0]
    ordered = (owner_rows % 2) * CB + owner_rows // 2
    hot = ordered[:, None] == lax.iota(jnp.int32, blk_devices)[None, :]
    count = hot.astype(jnp.int32)
    position = jnp.sum((jnp.cumsum(count, axis=0) - count) * count, axis=1)
    place_hot = position[:, None] == lax.iota(jnp.int32, STACKS_DEV)[None, :] // 2
    named = jnp.where(place_hot, (stack_slot + 1)[:, None], 0).astype(jnp.bfloat16)
    slots = lax.dot_general(
        hot.astype(jnp.bfloat16), named, (((0,), (0,)), ((), ())), preferred_element_type=jnp.float32
    )
    slots = slots.astype(jnp.int32) - 1
    outgoing = place_rows(ordered * CAP + position, keeps, gots, blk_devices * CAP)
    stacks = reduce_rows(outgoing, slots)
    lags = lax.iota(jnp.int32, HALF)
    turned = jnp.roll(stacks[:, ::-1], 1, axis=1)
    stacks = jnp.where(seg == 0, turned, stacks)
    return stacks.astype(jnp.bfloat16)


def solution(mesh):
    placed = (P("seg", "blk", None, None), P("blk", None), P("blk"))
    return jax.shard_map(
        local, mesh=mesh, in_specs=placed, out_specs=P("blk", "seg"), check_vma=False
    )
```

```python
import functools
import math

import jax
import jax.numpy as jnp
import numpy as np
from jax import lax
from jax.experimental import pallas as pl
from jax.experimental.pallas import tpu as pltpu
from jax.sharding import PartitionSpec as P

F = 2048
NFFT = 16384
LAGS = 512
HALF = LAGS // 2
WBAND = 128
STACKS_DEV = 128
CB = 64
SEGS = 8
PAIRS = CB * CB
CAP = 64
GROUP = 16
GROUPS = F // GROUP
WIDE = 128
VMEM = pl.BlockSpec(memory_space=pltpu.VMEM)
SMEM = pl.BlockSpec(memory_space=pltpu.SMEM)


def lag_rows(factor):
    bins = np.arange(1, F + 1)

    def phases(lags):
        wrapped = (np.asarray(lags)[:, None] * bins[None, :]) % NFFT
        return wrapped.astype(np.float32) * np.float32(2.0 * math.pi / NFFT)

    scale = np.float32(factor)
    last = np.zeros((16, F), np.float32)
    last[0] = np.cos(phases([HALF]))[0] * scale
    cos_rows = np.concatenate([np.cos(phases(np.arange(HALF))) * scale, last])
    sin_rows = np.sin(phases(np.concatenate([[HALF], np.arange(1, HALF)]))) * scale
    return cos_rows.astype(jnp.bfloat16), sin_rows.astype(jnp.bfloat16)


def whiten_kernel(x_ref, o_ref):
    lane = lax.broadcasted_iota(jnp.int32, (CB, WIDE), 1) // GROUP
    for band in range(F // WBAND):
        parts = []
        for part in range(2):
            first = part * F + band * WBAND
            parts.append([x_ref[s, :, first : first + WBAND].astype(jnp.float32) for s in range(4)])
        values = []
        scales = []
        for s in range(4):
            power = jnp.sum(parts[0][s] * parts[0][s] + parts[1][s] * parts[1][s], axis=1, keepdims=True)
            scales.append(lax.rsqrt(power * (1.0 / (2 * WBAND)) + 1e-06))
        for part in range(2):
            for s in range(4):
                values.append(parts[part][s] * scales[s])
        for step in (1, 2, 4):
            low = (lane // step) % 2 == 0
            swapped = list(values)
            for q in range(8):
                if q & step:
                    continue
                a, b = values[q], values[q + step]
                swapped[q] = jnp.where(low, a, pltpu.roll(b, GROUP * step, 1))
                swapped[q + step] = jnp.where(low, pltpu.roll(a, WIDE - GROUP * step, 1), b)
            values = swapped
        for g in range(8):
            first = (band * 8 + g) * WIDE
            o_ref[:, first : first + WIDE] = values[g].astype(jnp.bfloat16)


def whiten(spectra):
    return pl.pallas_call(
        whiten_kernel,
        out_shape=jax.ShapeDtypeStruct((CB, GROUPS * WIDE), jnp.bfloat16),
        in_specs=[VMEM],
        out_specs=VMEM,
        compiler_params=pltpu.CompilerParams(vmem_limit_bytes=12 * 2**20),
        cost_estimate=pl.CostEstimate(flops=20_000_000, bytes_accessed=2**22, transcendentals=4096),
        name="whiten",
    )(spectra.reshape(4, CB, 2 * F))


CHANS = 16
CHUNKS = CB // CHANS
CHUNK = CHANS * CB


def place_of(z, x, y, core):
    return ((z * 2 + x) * 4 + y) * 2 + core


def tile_kernel(
    own_ref, cos_ref, sin_ref, rows_ref,
    partner, g_re, g_im, keep, send, got, shift_send, shift_recv, swap_send, swap_recv,
):
    unroll = 32
    blk = lax.axis_index("blk")
    seg = lax.axis_index("seg")
    count = lax.axis_size("blk")
    ahead = ((blk + 1) % count, seg)
    behind = ((blk + count - 1) % count, seg)
    opposite = (blk, 1 - seg)
    barrier = pltpu.get_barrier_semaphore()
    for device in (ahead, behind, opposite):
        pl.semaphore_signal(barrier, inc=1, device_id=device, device_id_type=pl.DeviceIdType.MESH)
    pl.semaphore_wait(barrier, 3)

    def shift(j):
        at = pl.ds(pl.multiple_of(j * CHANS, CHANS), CHANS)
        return pltpu.make_async_remote_copy(
            src_ref=own_ref.at[at], dst_ref=partner.at[at],
            send_sem=shift_send.at[j], recv_sem=shift_recv.at[j],
            device_id=ahead, device_id_type=pl.DeviceIdType.MESH,
        )

    def swap(j):
        return pltpu.make_async_remote_copy(
            src_ref=send.at[j], dst_ref=got.at[j],
            send_sem=swap_send.at[j], recv_sem=swap_recv.at[j],
            device_id=opposite, device_id_type=pl.DeviceIdType.MESH,
        )

    for j in range(CHUNKS):
        shift(j).start()
    row = lax.broadcasted_iota(jnp.int32, (GROUP, WIDE), 0)
    lane = lax.broadcasted_iota(jnp.int32, (GROUP, WIDE), 1)
    kept = jnp.where(blk > 0, 1.0, 0.0)
    mask = jnp.where(row == lane % GROUP, kept, 0.0).astype(jnp.bfloat16)
    wide_lane = lax.broadcasted_iota(jnp.int32, (CB, WIDE), 1)
    turn = jnp.where(wide_lane < WIDE // 2, -1.0, 1.0).astype(jnp.bfloat16)
    top = lax.broadcasted_iota(jnp.int32, (HALF, 256), 0) == 0

    def chunk_step(j, carry):
        shift(j).wait()
        chan = pl.ds(pl.multiple_of(j * CHANS, CHANS), CHANS)

        def one(group):
            cols = pl.ds(pl.multiple_of(group * WIDE, WIDE), WIDE)
            own = own_ref[:, cols]
            turned = jnp.concatenate([own[:, CB:], own[:, :CB]], axis=1) * turn
            spread = jnp.broadcast_to(partner[chan, cols][:, None, :], (CHANS, GROUP, WIDE))
            out = lax.dot_general(
                (spread * mask[None]).reshape(CHANS * GROUP, WIDE),
                jnp.concatenate([own, turned], 0),
                (((1,), (1,)), ((), ())),
                preferred_element_type=jnp.float32,
            ).astype(jnp.bfloat16)
            rows = pl.ds(pl.multiple_of(group * GROUP, GROUP), GROUP)
            for i in range(CHANS // 2):
                first = out[2 * i * GROUP : (2 * i + 1) * GROUP]
                second = out[(2 * i + 1) * GROUP : (2 * i + 2) * GROUP]
                pair = slice(i * WIDE, (i + 1) * WIDE)
                g_re[rows, pair] = jnp.concatenate([first[:, :CB], second[:, :CB]], 1)
                g_im[rows, pair] = jnp.concatenate([first[:, CB:], second[:, CB:]], 1)

        def body(i, carry):
            for u in range(unroll):
                one(i * unroll + u)
            return carry

        lax.fori_loop(0, GROUPS // unroll, body, 0)
        for i in range(CHUNK // 256):
            cols = slice(i * 256, (i + 1) * 256)
            even = jnp.dot(cos_ref[...], g_re[:, cols], preferred_element_type=jnp.float32)
            odd = jnp.dot(sin_ref[...], g_im[:, cols], preferred_element_type=jnp.float32)
            low, last = even[:HALF], even[HALF : HALF + 1]
            before = jnp.where(top, last, low) + odd
            after = jnp.where(top, low, low - odd)
            keep[j, :, cols] = jnp.where(seg == 0, before, after)
            send[j, :, cols] = jnp.where(seg == 0, after, before).astype(jnp.bfloat16)
        swap(j).start()
        return carry

    lax.fori_loop(0, CHUNKS, chunk_step, 0)

    def finish_step(j, carry):
        swap(j).wait()
        for i in range(CHUNK // 256):
            cols = slice(i * 256, (i + 1) * 256)
            turned = (keep[j, :, cols] + got[j, :, cols].astype(jnp.float32)).T
            for side in range(2):
                at = pl.ds((j * CHUNK + i * 256) * 2 + side, 256, stride=2)
                rows_ref[at, :] = turned[:, side * WIDE : (side + 1) * WIDE]
        return carry

    lax.fori_loop(0, CHUNKS, finish_step, 0)


def tile_rows(own, cos_rows, sin_rows):
    return pl.pallas_call(
        tile_kernel,
        out_shape=jax.ShapeDtypeStruct((2 * PAIRS, WIDE), jnp.float32),
        in_specs=[VMEM, VMEM, VMEM],
        out_specs=VMEM,
        scratch_shapes=[
            pltpu.VMEM((CB, GROUPS * WIDE), jnp.bfloat16),
            pltpu.VMEM((F, CHUNK), jnp.bfloat16),
            pltpu.VMEM((F, CHUNK), jnp.bfloat16),
            pltpu.VMEM((CHUNKS, HALF, CHUNK), jnp.float32),
            pltpu.VMEM((CHUNKS, HALF, CHUNK), jnp.bfloat16),
            pltpu.VMEM((CHUNKS, HALF, CHUNK), jnp.bfloat16),
            pltpu.SemaphoreType.DMA((CHUNKS,)),
            pltpu.SemaphoreType.DMA((CHUNKS,)),
            pltpu.SemaphoreType.DMA((CHUNKS,)),
            pltpu.SemaphoreType.DMA((CHUNKS,)),
        ],
        compiler_params=pltpu.CompilerParams(
            collective_id=2, has_side_effects=True, vmem_limit_bytes=40 * 2**20
        ),
        cost_estimate=pl.CostEstimate(
            flops=25_000_000_000, bytes_accessed=2**24, transcendentals=0
        ),
        name="tiles",
    )(own, cos_rows, sin_rows)


def place_kernel(dest_ref, rows, out_ref, spread):
    def clear(i, carry):
        spread[pl.ds(pl.multiple_of(i * 512, 512), 512), :] = jnp.zeros((512, WIDE), jnp.float32)
        return carry

    lax.fori_loop(0, spread.shape[0] // 512, clear, 0)

    def move(i, carry):
        for u in range(64):
            p = i * 64 + u
            to = pl.multiple_of(dest_ref[p] * 2, 2)
            spread[pl.ds(to, 2), :] = rows[pl.ds(pl.multiple_of(p * 2, 2), 2), :]
        return carry

    lax.fori_loop(0, PAIRS // 64, move, 0)

    def finish(i, carry):
        at = pl.ds(pl.multiple_of(i * 512, 512), 512)
        out_ref[at, :] = spread[at, :].astype(jnp.bfloat16)
        return carry

    lax.fori_loop(0, spread.shape[0] // 512, finish, 0)


def place_rows(dest, rows, rows_out):
    return pl.pallas_call(
        place_kernel,
        out_shape=jax.ShapeDtypeStruct((2 * rows_out, WIDE), jnp.bfloat16),
        in_specs=[SMEM, VMEM],
        out_specs=VMEM,
        scratch_shapes=[pltpu.VMEM((2 * rows_out, WIDE), jnp.float32)],
        compiler_params=pltpu.CompilerParams(vmem_limit_bytes=24 * 2**20),
        name="place",
    )(dest, rows)


SLOTS_A, SLOTS_C, SLOTS_B = 48, 48, 32
AC = SLOTS_A + SLOTS_C


def reduce_kernel(
    rows_ref, slots_ref, out_ref,
    sib_rows, sib_slots, da, db, dc, ra, rb, rc, sa, sb, sc, ra2, rb2, rc2, t, tb, rt, rtb,
    send_sem, recv_sem,
):
    blk = lax.axis_index("blk")
    seg = lax.axis_index("seg")
    core = blk % 2
    y = (blk // 2) % 4
    x = (blk // 8) % 2
    z = blk // 16
    other = (place_of(z, x, y, 1 - core), seg)
    across = (place_of(z, 1 - x, y, core), seg)

    def along_y(k):
        return (place_of(z, x, (y + k) % 4, core), seg)

    def along_z(k):
        return (place_of((z + k) % 8, x, y, core), seg)

    partners = [other, across] + [along_y(k) for k in (1, 2, 3)] + [along_z(k) for k in range(1, 8)]
    barrier = pltpu.get_barrier_semaphore()
    for partner in partners:
        pl.semaphore_signal(barrier, inc=1, device_id=partner, device_id_type=pl.DeviceIdType.MESH)
    pl.semaphore_wait(barrier, len(partners))
    used = [0]

    def copy(src, dst, device):
        i = used[0]
        used[0] += 1
        made = pltpu.make_async_remote_copy(
            src_ref=src, dst_ref=dst, send_sem=send_sem.at[i], recv_sem=recv_sem.at[i],
            device_id=device, device_id_type=pl.DeviceIdType.MESH,
        )
        made.start()
        return made

    half = 2 * CB * CAP
    span = 2 * CAP
    order = [4, 3, 5, 2, 6, 1, 7, 0]
    named = copy(slots_ref.at[pl.ds((1 - core) * CB, CB)], sib_slots, other)
    swaps = {}
    for k in order:
        first = (z + k) % 8 * (8 * span)
        swaps[k] = copy(
            rows_ref.at[pl.ds((1 - core) * half + first, 8 * span)],
            sib_rows.at[pl.ds(first, 8 * span)],
            other,
        )
    named.wait()
    lane = lax.broadcasted_iota(jnp.int32, (1, 4 * CAP), 1)
    slot = lax.broadcasted_iota(jnp.int32, (STACKS_DEV, 4 * CAP), 0)

    def dense_one(i):
        zz, xx, yy = i // 8, (i // 4) % 2, i % 4
        names = jnp.concatenate([slots_ref[pl.ds(core * CB + i, 1), :], sib_slots[pl.ds(i, 1), :]], 1)
        left = jnp.where(lane % 2 == 0, names, -1)
        right = jnp.where(lane % 2 == 1, names, -1)
        hot = jnp.concatenate([slot == left, slot == right], 0)
        mine = rows_ref[pl.ds(pl.multiple_of(core * half + i * span, span), span), :]
        theirs = sib_rows[pl.ds(pl.multiple_of(i * span, span), span), :]
        total = jnp.dot(
            jnp.where(hot, 1.0, 0.0).astype(jnp.bfloat16),
            jnp.concatenate([mine, theirs], 0),
            preferred_element_type=jnp.float32,
        ).astype(jnp.bfloat16)
        total = jnp.concatenate([total[:STACKS_DEV], total[STACKS_DEV:]], 1)
        da[yy, zz, xx] = total[:SLOTS_A]
        dc[xx, zz, yy] = total[SLOTS_A:AC]
        db[zz, xx * 4 + yy] = total[AC:]

    def wide(value):
        return value.astype(jnp.float32)

    first_a, first_b, first_c, second_a, second_c, third = {}, {}, {}, {}, {}, {}
    for k in order:
        swaps[k].wait()
        there = (z + k) % 8

        def dense(i, carry, there=there):
            for u in range(4):
                dense_one(there * 8 + i * 4 + u)
            return carry

        lax.fori_loop(0, 2, dense, 0)
        first_c[k] = copy(dc.at[1 - x, there], rc.at[there], across)
        first_a[k] = [
            copy(da.at[(y + j) % 4, there], ra.at[j - 1, there], along_y(j)) for j in (2, 1, 3)
        ]
        if k:
            first_b[k] = copy(db.at[there], rb.at[k - 1], along_z(k))

    def second(k):
        there = (z + k) % 8
        first_c[k].wait()

        def sum_c(i, carry):
            sc[i, there] = (wide(dc[x, there, i]) + wide(rc[there, i])).astype(jnp.bfloat16)
            return carry

        lax.fori_loop(0, 4, sum_c, 0)
        second_c[k] = [
            copy(sc.at[(y + j) % 4, there], rc2.at[j - 1, there], along_y(j)) for j in (2, 1, 3)
        ]
        for made in first_a[k]:
            made.wait()

        def sum_a(i, carry):
            total = wide(da[y, there, i])
            for j in range(3):
                total += wide(ra[j, there, i])
            sa[i, there] = total.astype(jnp.bfloat16)
            return carry

        lax.fori_loop(0, 2, sum_a, 0)
        second_a[k] = copy(sa.at[1 - x, there], ra2.at[there], across)

    def finish(k):
        there = (z + k) % 8
        second_a[k].wait()
        t[there, :SLOTS_A] = (wide(sa[x, there]) + wide(ra2[there])).astype(jnp.bfloat16)
        for made in second_c[k]:
            made.wait()
        total = wide(sc[y, there])
        for j in range(3):
            total += wide(rc2[j, there])
        t[there, SLOTS_A:] = total.astype(jnp.bfloat16)
        if k:
            third[k] = copy(t.at[there], rt.at[k - 1], along_z(k))

    late = 2
    for n, k in enumerate(order):
        second(k)
        if n >= late:
            finish(order[n - late])
    for made in first_b.values():
        made.wait()

    def sum_b(i, carry):
        total = wide(db[z, i])
        for k in range(7):
            total += wide(rb[k, i])
        sb[i % 4, i // 4] = total.astype(jnp.bfloat16)
        return carry

    lax.fori_loop(0, 8, sum_b, 0)
    second_b = [copy(sb.at[(y + k) % 4], rb2.at[k - 1], along_y(k)) for k in (1, 2, 3)]
    for k in order[-late:]:
        finish(k)
    for made in second_b:
        made.wait()

    def sum_b2(i, carry):
        total = wide(sb[y, i])
        for k in range(3):
            total += wide(rb2[k, i])
        tb[i] = total.astype(jnp.bfloat16)
        return carry

    lax.fori_loop(0, 2, sum_b2, 0)
    third_b = copy(tb.at[1 - x], rtb, across)
    total = wide(t[z])
    for k in order[:-1]:
        third[k].wait()
        total += wide(rt[k - 1])
    out_ref[:AC, :] = total
    third_b.wait()
    out_ref[AC:, :] = wide(tb[x]) + wide(rtb[...])


def reduce_rows(rows, slots):
    def buf(*shape):
        return pltpu.VMEM((*shape, HALF), jnp.bfloat16)

    a, b, c = SLOTS_A, SLOTS_B, SLOTS_C
    count = 9 + 8 + 24 + 7 + 24 + 8 + 7 + 3 + 1
    return pl.pallas_call(
        reduce_kernel,
        out_shape=jax.ShapeDtypeStruct((STACKS_DEV, HALF), jnp.float32),
        in_specs=[VMEM, VMEM],
        out_specs=VMEM,
        scratch_shapes=[
            pltpu.VMEM((2 * CB * CAP, WIDE), jnp.bfloat16), pltpu.VMEM((CB, STACKS_DEV), jnp.int32),
            buf(4, 8, 2, a), buf(8, 8, b), buf(2, 8, 4, c), buf(3, 8, 2, a), buf(7, 8, b), buf(8, 4, c),
            buf(2, 8, a), buf(4, 2, b), buf(4, 8, c), buf(8, a), buf(3, 2, b), buf(3, 8, c),
            buf(8, AC), buf(2, b), buf(7, AC), buf(b),
            pltpu.SemaphoreType.DMA((count,)), pltpu.SemaphoreType.DMA((count,)),
        ],
        compiler_params=pltpu.CompilerParams(
            collective_id=1, has_side_effects=True, vmem_limit_bytes=40 * 2**20
        ),
        cost_estimate=pl.CostEstimate(flops=2_000_000_000, bytes_accessed=2**23, transcendentals=0),
        name="reduce_rows",
    )(rows, slots)


def local(spectra, owner_device, stack_slot):
    blk_devices = lax.axis_size("blk")
    seg = lax.axis_index("seg")
    factor = (2.0 * F * SEGS) ** (-0.5)
    cos_rows, sin_rows = lag_rows(factor)
    rows = tile_rows(whiten(spectra), cos_rows, sin_rows)
    owner_rows = owner_device[:, 0]
    ordered = (owner_rows % 2) * CB + owner_rows // 2
    hot = ordered[:, None] == lax.iota(jnp.int32, blk_devices)[None, :]
    count = hot.astype(jnp.int32)
    position = jnp.sum((jnp.cumsum(count, axis=0) - count) * count, axis=1)
    place_hot = position[:, None] == lax.iota(jnp.int32, STACKS_DEV)[None, :] // 2
    named = jnp.where(place_hot, (stack_slot + 1)[:, None], 0).astype(jnp.bfloat16)
    slots = lax.dot_general(
        hot.astype(jnp.bfloat16), named, (((0,), (0,)), ((), ())), preferred_element_type=jnp.float32
    )
    slots = slots.astype(jnp.int32) - 1
    outgoing = place_rows(ordered * CAP + position, rows, blk_devices * CAP)
    stacks = reduce_rows(outgoing, slots)
    lags = lax.iota(jnp.int32, HALF)
    turned = jnp.roll(stacks[:, ::-1], 1, axis=1)
    stacks = jnp.where(seg == 0, turned, stacks)
    return stacks.astype(jnp.bfloat16)


def solution(mesh):
    placed = (P("seg", "blk", None, None), P("blk", None), P("blk"))
    return jax.shard_map(
        local, mesh=mesh, in_specs=placed, out_specs=P("blk", "seg"), check_vma=False
    )
```

```python
import functools
import math

import jax
import jax.numpy as jnp
import numpy as np
from jax import lax
from jax.experimental import pallas as pl
from jax.experimental.pallas import tpu as pltpu
from jax.sharding import PartitionSpec as P

F = 2048
NFFT = 16384
LAGS = 512
HALF = LAGS // 2
WBAND = 128
STACKS_DEV = 128
CB = 64
SEGS = 8
PAIRS = CB * CB
CAP = 64
GROUP = 16
GROUPS = F // GROUP
WIDE = 128
VMEM = pl.BlockSpec(memory_space=pltpu.VMEM)
SMEM = pl.BlockSpec(memory_space=pltpu.SMEM)


def lag_rows(factor):
    bins = np.arange(1, F + 1)

    def phases(lags):
        wrapped = (np.asarray(lags)[:, None] * bins[None, :]) % NFFT
        return wrapped.astype(np.float32) * np.float32(2.0 * math.pi / NFFT)

    scale = np.float32(factor)
    last = np.zeros((16, F), np.float32)
    last[0] = np.cos(phases([HALF]))[0] * scale
    cos_rows = np.concatenate([np.cos(phases(np.arange(HALF))) * scale, last])
    sin_rows = np.sin(phases(np.concatenate([[HALF], np.arange(1, HALF)]))) * scale
    return cos_rows.astype(jnp.bfloat16), sin_rows.astype(jnp.bfloat16)


def whiten_kernel(x_ref, o_ref):
    lane = lax.broadcasted_iota(jnp.int32, (CB, WIDE), 1) // GROUP
    for band in range(F // WBAND):
        parts = []
        for part in range(2):
            first = part * F + band * WBAND
            parts.append([x_ref[s, :, first : first + WBAND].astype(jnp.float32) for s in range(4)])
        values = []
        scales = []
        for s in range(4):
            power = jnp.sum(parts[0][s] * parts[0][s] + parts[1][s] * parts[1][s], axis=1, keepdims=True)
            scales.append(lax.rsqrt(power * (1.0 / (2 * WBAND)) + 1e-06))
        for part in range(2):
            for s in range(4):
                values.append(parts[part][s] * scales[s])
        for step in (1, 2, 4):
            low = (lane // step) % 2 == 0
            swapped = list(values)
            for q in range(8):
                if q & step:
                    continue
                a, b = values[q], values[q + step]
                swapped[q] = jnp.where(low, a, pltpu.roll(b, GROUP * step, 1))
                swapped[q + step] = jnp.where(low, pltpu.roll(a, WIDE - GROUP * step, 1), b)
            values = swapped
        for g in range(8):
            first = (band * 8 + g) * WIDE
            o_ref[:, first : first + WIDE] = values[g].astype(jnp.bfloat16)


def whiten(spectra):
    return pl.pallas_call(
        whiten_kernel,
        out_shape=jax.ShapeDtypeStruct((CB, GROUPS * WIDE), jnp.bfloat16),
        in_specs=[VMEM],
        out_specs=VMEM,
        compiler_params=pltpu.CompilerParams(vmem_limit_bytes=12 * 2**20),
        cost_estimate=pl.CostEstimate(flops=20_000_000, bytes_accessed=2**22, transcendentals=4096),
        name="whiten",
    )(spectra.reshape(4, CB, 2 * F))


CHANS = 16
CHUNKS = CB // CHANS
CHUNK = CHANS * CB


def place_of(z, x, y, core):
    return ((z * 2 + x) * 4 + y) * 2 + core


def tile_kernel(
    own_ref, cos_ref, sin_ref, owner_ref, slot_ref, rows_ref, dest_ref, slots_ref,
    partner, g_re, g_im, keep, send, got, passing, shift_send, shift_recv, swap_send, swap_recv, pass_send, pass_recv,
):
    unroll = 32
    blk = lax.axis_index("blk")
    seg = lax.axis_index("seg")
    count = lax.axis_size("blk")
    ahead = ((blk + 1) % count, seg)
    behind = ((blk + count - 1) % count, seg)
    opposite = (blk, 1 - seg)
    core = blk % 2
    y = (blk // 2) % 4
    x = (blk // 8) % 2
    z = blk // 16
    turns = jnp.logical_and(y == 3, core == 1)
    lands = jnp.logical_and(y == 0, core == 0)
    relays = jnp.logical_and(jnp.logical_or(y == 1, y == 2), core == 1)
    origin = place_of(z, x, 3, 1)
    target = ((origin + 1) % count, seg)
    back = (blk + count - 1) % count
    barrier = pltpu.get_barrier_semaphore()

    def greet(device):
        pl.semaphore_signal(barrier, inc=1, device_id=device, device_id_type=pl.DeviceIdType.MESH)

    for device in (ahead, behind, opposite):
        greet(device)

    @pl.when(turns)
    def _():
        greet((place_of(z, x, 1, 1), seg))
        greet((place_of(z, x, 2, 1), seg))

    @pl.when(relays)
    def _():
        greet((origin, seg))
        greet(target)

    @pl.when(lands)
    def _():
        greet((place_of(back // 16, (back // 8) % 2, 1, 1), seg))
        greet((place_of(back // 16, (back // 8) % 2, 2, 1), seg))

    special = jnp.logical_or(jnp.logical_or(turns, lands), relays)
    pl.semaphore_wait(barrier, jnp.where(special, 5, 3))

    def detour(j):
        at = pl.ds(pl.multiple_of(j * CHANS, CHANS), CHANS)
        return pltpu.make_async_remote_copy(
            src_ref=own_ref.at[at], dst_ref=passing,
            send_sem=shift_send.at[j], recv_sem=pass_recv,
            device_id=(place_of(z, x, j - 1, 1), seg), device_id_type=pl.DeviceIdType.MESH,
        )

    def forward(j):
        at = pl.ds(pl.multiple_of(j * CHANS, CHANS), CHANS)
        return pltpu.make_async_remote_copy(
            src_ref=passing, dst_ref=partner.at[at],
            send_sem=pass_send, recv_sem=shift_recv.at[j],
            device_id=target, device_id_type=pl.DeviceIdType.MESH,
        )

    def shift(j):
        at = pl.ds(pl.multiple_of(j * CHANS, CHANS), CHANS)
        return pltpu.make_async_remote_copy(
            src_ref=own_ref.at[at], dst_ref=partner.at[at],
            send_sem=shift_send.at[j], recv_sem=shift_recv.at[j],
            device_id=ahead, device_id_type=pl.DeviceIdType.MESH,
        )

    def swap(j):
        return pltpu.make_async_remote_copy(
            src_ref=send.at[j], dst_ref=got.at[j],
            send_sem=swap_send.at[j], recv_sem=swap_recv.at[j],
            device_id=opposite, device_id_type=pl.DeviceIdType.MESH,
        )

    @pl.when(turns)
    def _():
        for j in range(CHUNKS // 2, CHUNKS):
            detour(j).start()

    for j in range(CHUNKS // 2):
        shift(j).start()

    @pl.when(jnp.logical_not(turns))
    def _():
        for j in range(CHUNKS // 2, CHUNKS):
            shift(j).start()

    for j in range(CHUNKS // 2, CHUNKS):

        @pl.when(jnp.logical_and(relays, y == j - 1))
        def _(j=j):
            detour(j).wait_recv()
            forward(j).start()

    row = lax.broadcasted_iota(jnp.int32, (GROUP, WIDE), 0)
    lane = lax.broadcasted_iota(jnp.int32, (GROUP, WIDE), 1)
    kept = jnp.where(blk > 0, 1.0, 0.0)
    mask = jnp.where(row == lane % GROUP, kept, 0.0).astype(jnp.bfloat16)
    wide_lane = lax.broadcasted_iota(jnp.int32, (CB, WIDE), 1)
    turn = jnp.where(wide_lane < WIDE // 2, -1.0, 1.0).astype(jnp.bfloat16)
    top = lax.broadcasted_iota(jnp.int32, (HALF, 256), 0) == 0

    def chunk_step(j, carry):
        shift(j).wait()
        chan = pl.ds(pl.multiple_of(j * CHANS, CHANS), CHANS)

        def one(group):
            cols = pl.ds(pl.multiple_of(group * WIDE, WIDE), WIDE)
            own = own_ref[:, cols]
            turned = jnp.concatenate([own[:, CB:], own[:, :CB]], axis=1) * turn
            spread = jnp.broadcast_to(partner[chan, cols][:, None, :], (CHANS, GROUP, WIDE))
            out = lax.dot_general(
                (spread * mask[None]).reshape(CHANS * GROUP, WIDE),
                jnp.concatenate([own, turned], 0),
                (((1,), (1,)), ((), ())),
                preferred_element_type=jnp.float32,
            ).astype(jnp.bfloat16)
            rows = pl.ds(pl.multiple_of(group * GROUP, GROUP), GROUP)
            for i in range(CHANS // 2):
                first = out[2 * i * GROUP : (2 * i + 1) * GROUP]
                second = out[(2 * i + 1) * GROUP : (2 * i + 2) * GROUP]
                pair = slice(i * WIDE, (i + 1) * WIDE)
                g_re[rows, pair] = jnp.concatenate([first[:, :CB], second[:, :CB]], 1)
                g_im[rows, pair] = jnp.concatenate([first[:, CB:], second[:, CB:]], 1)

        def body(i, carry):
            for u in range(unroll):
                one(i * unroll + u)
            return carry

        lax.fori_loop(0, GROUPS // unroll, body, 0)
        for i in range(CHUNK // 256):
            cols = slice(i * 256, (i + 1) * 256)
            even = jnp.dot(cos_ref[...], g_re[:, cols], preferred_element_type=jnp.float32)
            odd = jnp.dot(sin_ref[...], g_im[:, cols], preferred_element_type=jnp.float32)
            low, last = even[:HALF], even[HALF : HALF + 1]
            before = jnp.where(top, last, low) + odd
            after = jnp.where(top, low, low - odd)
            keep[j, :, cols] = jnp.where(seg == 0, before, after)
            send[j, :, cols] = jnp.where(seg == 0, after, before).astype(jnp.bfloat16)
        swap(j).start()
        return carry

    lax.fori_loop(0, CHUNKS, chunk_step, 0)

    row_of = lax.broadcasted_iota(jnp.int32, (256, 256), 0)
    upper = jnp.where(row_of < lax.broadcasted_iota(jnp.int32, (256, 256), 1), 1.0, 0.0)
    upper = upper.astype(jnp.bfloat16)
    owner_row = lax.broadcasted_iota(jnp.int32, (STACKS_DEV, 256), 0)

    def index_step(i, carry):
        seen, named = carry
        at = pl.ds(pl.multiple_of(i * 256, 256), 256)
        owner = owner_ref[:, at]
        ordered = owner % 2 * CB + owner // 2
        hot = jnp.where(owner_row == ordered, 1.0, 0.0)
        before = jnp.dot(hot.astype(jnp.bfloat16), upper, preferred_element_type=jnp.float32) + seen
        position = jnp.sum(hot * before, axis=0, keepdims=True).astype(jnp.int32)
        dest_ref[:, at] = ordered * CAP + position
        names = jnp.where(owner_row // 2 == position, (slot_ref[:, at] + 1).astype(jnp.float32), 0.0)
        named += lax.dot_general(
            hot.astype(jnp.bfloat16),
            names.astype(jnp.bfloat16),
            (((1,), (1,)), ((), ())),
            preferred_element_type=jnp.float32,
        )
        return seen + jnp.sum(hot, axis=1, keepdims=True), named

    _, named = lax.fori_loop(
        0,
        PAIRS // 256,
        index_step,
        (jnp.zeros((STACKS_DEV, 1), jnp.float32), jnp.zeros((STACKS_DEV, STACKS_DEV), jnp.float32)),
    )
    slots_ref[...] = named.astype(jnp.int32) - 1

    def finish_step(j, carry):
        swap(j).wait()
        for i in range(CHUNK // 256):
            cols = slice(i * 256, (i + 1) * 256)
            turned = (keep[j, :, cols] + got[j, :, cols].astype(jnp.float32)).T
            for side in range(2):
                at = pl.ds((j * CHUNK + i * 256) * 2 + side, 256, stride=2)
                rows_ref[at, :] = turned[:, side * WIDE : (side + 1) * WIDE]
        return carry

    lax.fori_loop(0, CHUNKS, finish_step, 0)
    for j in range(CHUNKS // 2, CHUNKS):

        @pl.when(jnp.logical_and(relays, y == j - 1))
        def _(j=j):
            forward(j).wait_send()


def tile_rows(own, cos_rows, sin_rows, owner, slot):
    return pl.pallas_call(
        tile_kernel,
        out_shape=(
            jax.ShapeDtypeStruct((2 * PAIRS, WIDE), jnp.float32),
            jax.ShapeDtypeStruct((1, PAIRS), jnp.int32),
            jax.ShapeDtypeStruct((STACKS_DEV, STACKS_DEV), jnp.int32),
        ),
        in_specs=[VMEM] * 5,
        out_specs=(VMEM, VMEM, VMEM),
        scratch_shapes=[
            pltpu.VMEM((CB, GROUPS * WIDE), jnp.bfloat16),
            pltpu.VMEM((F, CHUNK), jnp.bfloat16),
            pltpu.VMEM((F, CHUNK), jnp.bfloat16),
            pltpu.VMEM((CHUNKS, HALF, CHUNK), jnp.float32),
            pltpu.VMEM((CHUNKS, HALF, CHUNK), jnp.bfloat16),
            pltpu.VMEM((CHUNKS, HALF, CHUNK), jnp.bfloat16),
            pltpu.VMEM((CHANS, GROUPS * WIDE), jnp.bfloat16),
            pltpu.SemaphoreType.DMA((CHUNKS,)),
            pltpu.SemaphoreType.DMA((CHUNKS,)),
            pltpu.SemaphoreType.DMA((CHUNKS,)),
            pltpu.SemaphoreType.DMA((CHUNKS,)),
            pltpu.SemaphoreType.DMA,
            pltpu.SemaphoreType.DMA,
        ],
        compiler_params=pltpu.CompilerParams(
            collective_id=2, has_side_effects=True, vmem_limit_bytes=40 * 2**20
        ),
        cost_estimate=pl.CostEstimate(
            flops=25_000_000_000, bytes_accessed=2**24, transcendentals=0
        ),
        name="tiles",
    )(own, cos_rows, sin_rows, owner, slot)


def place_kernel(dest_ref, rows, out_ref, spread):
    def clear(i, carry):
        spread[pl.ds(pl.multiple_of(i * 512, 512), 512), :] = jnp.zeros((512, WIDE), jnp.float32)
        return carry

    lax.fori_loop(0, spread.shape[0] // 512, clear, 0)

    def move(i, carry):
        for u in range(64):
            p = i * 64 + u
            to = pl.multiple_of(dest_ref[p] * 2, 2)
            spread[pl.ds(to, 2), :] = rows[pl.ds(pl.multiple_of(p * 2, 2), 2), :]
        return carry

    lax.fori_loop(0, PAIRS // 64, move, 0)

    def finish(i, carry):
        at = pl.ds(pl.multiple_of(i * 512, 512), 512)
        out_ref[at, :] = spread[at, :].astype(jnp.bfloat16)
        return carry

    lax.fori_loop(0, spread.shape[0] // 512, finish, 0)


def place_rows(dest, rows, rows_out):
    return pl.pallas_call(
        place_kernel,
        out_shape=jax.ShapeDtypeStruct((2 * rows_out, WIDE), jnp.bfloat16),
        in_specs=[SMEM, VMEM],
        out_specs=VMEM,
        scratch_shapes=[pltpu.VMEM((2 * rows_out, WIDE), jnp.float32)],
        compiler_params=pltpu.CompilerParams(vmem_limit_bytes=24 * 2**20),
        name="place",
    )(dest, rows)


SLOTS_A, SLOTS_C, SLOTS_B = 48, 48, 32
AC = SLOTS_A + SLOTS_C


def reduce_kernel(
    rows_ref, slots_ref, out_ref,
    sib_rows, sib_slots, da, db, dc, ra, rb, rc, sa, sb, sc, ra2, rb2, rc2, t, tb, rt, rtb,
    send_sem, recv_sem,
):
    blk = lax.axis_index("blk")
    seg = lax.axis_index("seg")
    core = blk % 2
    y = (blk // 2) % 4
    x = (blk // 8) % 2
    z = blk // 16
    other = (place_of(z, x, y, 1 - core), seg)
    across = (place_of(z, 1 - x, y, core), seg)

    def along_y(k):
        return (place_of(z, x, (y + k) % 4, core), seg)

    def along_z(k):
        return (place_of((z + k) % 8, x, y, core), seg)

    partners = [other, across] + [along_y(k) for k in (1, 2, 3)] + [along_z(k) for k in range(1, 8)]
    barrier = pltpu.get_barrier_semaphore()
    for partner in partners:
        pl.semaphore_signal(barrier, inc=1, device_id=partner, device_id_type=pl.DeviceIdType.MESH)
    pl.semaphore_wait(barrier, len(partners))
    used = [0]

    def copy(src, dst, device):
        i = used[0]
        used[0] += 1
        made = pltpu.make_async_remote_copy(
            src_ref=src, dst_ref=dst, send_sem=send_sem.at[i], recv_sem=recv_sem.at[i],
            device_id=device, device_id_type=pl.DeviceIdType.MESH,
        )
        made.start()
        return made

    half = 2 * CB * CAP
    span = 2 * CAP
    order = [4, 3, 5, 2, 6, 1, 7, 0]
    named = copy(slots_ref.at[pl.ds((1 - core) * CB, CB)], sib_slots, other)
    swaps = {}
    for k in order:
        first = (z + k) % 8 * (8 * span)
        swaps[k] = copy(
            rows_ref.at[pl.ds((1 - core) * half + first, 8 * span)],
            sib_rows.at[pl.ds(first, 8 * span)],
            other,
        )
    named.wait()
    lane = lax.broadcasted_iota(jnp.int32, (1, 4 * CAP), 1)
    slot = lax.broadcasted_iota(jnp.int32, (STACKS_DEV, 4 * CAP), 0)

    def dense_one(i):
        zz, xx, yy = i // 8, (i // 4) % 2, i % 4
        names = jnp.concatenate([slots_ref[pl.ds(core * CB + i, 1), :], sib_slots[pl.ds(i, 1), :]], 1)
        left = jnp.where(lane % 2 == 0, names, -1)
        right = jnp.where(lane % 2 == 1, names, -1)
        hot = jnp.concatenate([slot == left, slot == right], 0)
        mine = rows_ref[pl.ds(pl.multiple_of(core * half + i * span, span), span), :]
        theirs = sib_rows[pl.ds(pl.multiple_of(i * span, span), span), :]
        total = jnp.dot(
            jnp.where(hot, 1.0, 0.0).astype(jnp.bfloat16),
            jnp.concatenate([mine, theirs], 0),
            preferred_element_type=jnp.float32,
        ).astype(jnp.bfloat16)
        total = jnp.concatenate([total[:STACKS_DEV], total[STACKS_DEV:]], 1)
        da[yy, zz, xx] = total[:SLOTS_A]
        dc[xx, zz, yy] = total[SLOTS_A:AC]
        db[zz, xx * 4 + yy] = total[AC:]

    def wide(value):
        return value.astype(jnp.float32)

    first_a, first_b, first_c, second_a, second_c, third = {}, {}, {}, {}, {}, {}
    for k in order:
        swaps[k].wait()
        there = (z + k) % 8

        def dense(i, carry, there=there):
            for u in range(4):
                dense_one(there * 8 + i * 4 + u)
            return carry

        lax.fori_loop(0, 2, dense, 0)
        first_c[k] = copy(dc.at[1 - x, there], rc.at[there], across)
        first_a[k] = [
            copy(da.at[(y + j) % 4, there], ra.at[j - 1, there], along_y(j)) for j in (2, 1, 3)
        ]
        if k:
            first_b[k] = copy(db.at[there], rb.at[k - 1], along_z(k))

    def second(k):
        there = (z + k) % 8
        first_c[k].wait()

        def sum_c(i, carry):
            sc[i, there] = (wide(dc[x, there, i]) + wide(rc[there, i])).astype(jnp.bfloat16)
            return carry

        lax.fori_loop(0, 4, sum_c, 0)
        second_c[k] = [
            copy(sc.at[(y + j) % 4, there], rc2.at[j - 1, there], along_y(j)) for j in (2, 1, 3)
        ]
        for made in first_a[k]:
            made.wait()

        def sum_a(i, carry):
            total = wide(da[y, there, i])
            for j in range(3):
                total += wide(ra[j, there, i])
            sa[i, there] = total.astype(jnp.bfloat16)
            return carry

        lax.fori_loop(0, 2, sum_a, 0)
        second_a[k] = copy(sa.at[1 - x, there], ra2.at[there], across)

    def finish(k):
        there = (z + k) % 8
        second_a[k].wait()
        t[there, :SLOTS_A] = (wide(sa[x, there]) + wide(ra2[there])).astype(jnp.bfloat16)
        for made in second_c[k]:
            made.wait()
        total = wide(sc[y, there])
        for j in range(3):
            total += wide(rc2[j, there])
        t[there, SLOTS_A:] = total.astype(jnp.bfloat16)
        if k:
            third[k] = copy(t.at[there], rt.at[k - 1], along_z(k))

    late = 2
    for n, k in enumerate(order):
        second(k)
        if n >= late:
            finish(order[n - late])
    for made in first_b.values():
        made.wait()

    def sum_b(i, carry):
        total = wide(db[z, i])
        for k in range(7):
            total += wide(rb[k, i])
        sb[i % 4, i // 4] = total.astype(jnp.bfloat16)
        return carry

    lax.fori_loop(0, 8, sum_b, 0)
    second_b = [copy(sb.at[(y + k) % 4], rb2.at[k - 1], along_y(k)) for k in (1, 2, 3)]
    for k in order[-late:]:
        finish(k)
    for made in second_b:
        made.wait()

    def sum_b2(i, carry):
        total = wide(sb[y, i])
        for k in range(3):
            total += wide(rb2[k, i])
        tb[i] = total.astype(jnp.bfloat16)
        return carry

    lax.fori_loop(0, 2, sum_b2, 0)
    third_b = copy(tb.at[1 - x], rtb, across)
    total = wide(t[z])
    for k in order[:-1]:
        third[k].wait()
        total += wide(rt[k - 1])
    out_ref[:AC, :] = total
    third_b.wait()
    out_ref[AC:, :] = wide(tb[x]) + wide(rtb[...])


def reduce_rows(rows, slots):
    def buf(*shape):
        return pltpu.VMEM((*shape, HALF), jnp.bfloat16)

    a, b, c = SLOTS_A, SLOTS_B, SLOTS_C
    count = 9 + 8 + 24 + 7 + 24 + 8 + 7 + 3 + 1
    return pl.pallas_call(
        reduce_kernel,
        out_shape=jax.ShapeDtypeStruct((STACKS_DEV, HALF), jnp.float32),
        in_specs=[VMEM, VMEM],
        out_specs=VMEM,
        scratch_shapes=[
            pltpu.VMEM((2 * CB * CAP, WIDE), jnp.bfloat16), pltpu.VMEM((CB, STACKS_DEV), jnp.int32),
            buf(4, 8, 2, a), buf(8, 8, b), buf(2, 8, 4, c), buf(3, 8, 2, a), buf(7, 8, b), buf(8, 4, c),
            buf(2, 8, a), buf(4, 2, b), buf(4, 8, c), buf(8, a), buf(3, 2, b), buf(3, 8, c),
            buf(8, AC), buf(2, b), buf(7, AC), buf(b),
            pltpu.SemaphoreType.DMA((count,)), pltpu.SemaphoreType.DMA((count,)),
        ],
        compiler_params=pltpu.CompilerParams(
            collective_id=1, has_side_effects=True, vmem_limit_bytes=40 * 2**20
        ),
        cost_estimate=pl.CostEstimate(flops=2_000_000_000, bytes_accessed=2**23, transcendentals=0),
        name="reduce_rows",
    )(rows, slots)


def local(spectra, owner_device, stack_slot):
    blk_devices = lax.axis_size("blk")
    seg = lax.axis_index("seg")
    factor = (2.0 * F * SEGS) ** (-0.5)
    cos_rows, sin_rows = lag_rows(factor)
    rows, dest, slots = tile_rows(
        whiten(spectra),
        cos_rows,
        sin_rows,
        owner_device.reshape(1, PAIRS),
        stack_slot.reshape(1, PAIRS),
    )
    outgoing = place_rows(dest.reshape(PAIRS), rows, blk_devices * CAP)
    stacks = reduce_rows(outgoing, slots)
    lags = lax.iota(jnp.int32, HALF)
    turned = jnp.roll(stacks[:, ::-1], 1, axis=1)
    stacks = jnp.where(seg == 0, turned, stacks)
    return stacks.astype(jnp.bfloat16)


def solution(mesh):
    placed = (P("seg", "blk", None, None), P("blk", None), P("blk"))
    return jax.shard_map(
        local, mesh=mesh, in_specs=placed, out_specs=P("blk", "seg"), check_vma=False
    )
```

```python
import functools
import math

import jax
import jax.numpy as jnp
import numpy as np
from jax import lax
from jax.experimental import pallas as pl
from jax.experimental.pallas import tpu as pltpu
from jax.sharding import PartitionSpec as P

F = 2048
NFFT = 16384
LAGS = 512
HALF = LAGS // 2
WBAND = 128
STACKS_DEV = 128
CB = 64
SEGS = 8
PAIRS = CB * CB
CAP = 64
GROUP = 16
GROUPS = F // GROUP
WIDE = 128
VMEM = pl.BlockSpec(memory_space=pltpu.VMEM)
SMEM = pl.BlockSpec(memory_space=pltpu.SMEM)


def lag_rows(factor):
    bins = np.arange(1, F + 1)

    def phases(lags):
        wrapped = (np.asarray(lags)[:, None] * bins[None, :]) % NFFT
        return wrapped.astype(np.float32) * np.float32(2.0 * math.pi / NFFT)

    scale = np.float32(factor)
    last = np.zeros((16, F), np.float32)
    last[0] = np.cos(phases([HALF]))[0] * scale
    cos_rows = np.concatenate([np.cos(phases(np.arange(HALF))) * scale, last])
    sin_rows = np.sin(phases(np.concatenate([[HALF], np.arange(1, HALF)]))) * scale
    return cos_rows.astype(jnp.bfloat16), sin_rows.astype(jnp.bfloat16)


def whiten_kernel(x_ref, o_ref):
    lane = lax.broadcasted_iota(jnp.int32, (CB, WIDE), 1) // GROUP
    for band in range(F // WBAND):
        parts = []
        for part in range(2):
            first = part * F + band * WBAND
            parts.append([x_ref[s, :, first : first + WBAND].astype(jnp.float32) for s in range(4)])
        values = []
        scales = []
        for s in range(4):
            power = jnp.sum(parts[0][s] * parts[0][s] + parts[1][s] * parts[1][s], axis=1, keepdims=True)
            scales.append(lax.rsqrt(power * (1.0 / (2 * WBAND)) + 1e-06))
        for part in range(2):
            for s in range(4):
                values.append(parts[part][s] * scales[s])
        for step in (1, 2, 4):
            low = (lane // step) % 2 == 0
            swapped = list(values)
            for q in range(8):
                if q & step:
                    continue
                a, b = values[q], values[q + step]
                swapped[q] = jnp.where(low, a, pltpu.roll(b, GROUP * step, 1))
                swapped[q + step] = jnp.where(low, pltpu.roll(a, WIDE - GROUP * step, 1), b)
            values = swapped
        for g in range(8):
            first = (band * 8 + g) * WIDE
            o_ref[:, first : first + WIDE] = values[g].astype(jnp.bfloat16)


def whiten(spectra):
    return pl.pallas_call(
        whiten_kernel,
        out_shape=jax.ShapeDtypeStruct((CB, GROUPS * WIDE), jnp.bfloat16),
        in_specs=[VMEM],
        out_specs=VMEM,
        compiler_params=pltpu.CompilerParams(vmem_limit_bytes=12 * 2**20),
        cost_estimate=pl.CostEstimate(flops=20_000_000, bytes_accessed=2**22, transcendentals=4096),
        name="whiten",
    )(spectra.reshape(4, CB, 2 * F))


CHANS = 16
CHUNKS = CB // CHANS
CHUNK = CHANS * CB


def place_of(z, x, y, core):
    return ((z * 2 + x) * 4 + y) * 2 + core


def tile_kernel(
    own_ref, cos_ref, sin_ref, owner_ref, slot_ref, rows_ref, dest_ref, slots_ref,
    partner, g_re, g_im, keep, send, got, passing, shift_send, shift_recv, swap_send, swap_recv, pass_send, pass_recv,
):
    unroll = 32
    blk = lax.axis_index("blk")
    seg = lax.axis_index("seg")
    count = lax.axis_size("blk")
    ahead = ((blk + 1) % count, seg)
    behind = ((blk + count - 1) % count, seg)
    opposite = (blk, 1 - seg)
    core = blk % 2
    y = (blk // 2) % 4
    x = (blk // 8) % 2
    z = blk // 16
    turns = jnp.logical_and(y == 3, core == 1)
    lands = jnp.logical_and(y == 0, core == 0)
    relays = jnp.logical_and(jnp.logical_or(y == 1, y == 2), core == 1)
    origin = place_of(z, x, 3, 1)
    target = ((origin + 1) % count, seg)
    back = (blk + count - 1) % count
    barrier = pltpu.get_barrier_semaphore()

    def greet(device):
        pl.semaphore_signal(barrier, inc=1, device_id=device, device_id_type=pl.DeviceIdType.MESH)

    for device in (ahead, behind, opposite):
        greet(device)

    @pl.when(turns)
    def _():
        greet((place_of(z, x, 1, 1), seg))
        greet((place_of(z, x, 2, 1), seg))

    @pl.when(relays)
    def _():
        greet((origin, seg))
        greet(target)

    @pl.when(lands)
    def _():
        greet((place_of(back // 16, (back // 8) % 2, 1, 1), seg))
        greet((place_of(back // 16, (back // 8) % 2, 2, 1), seg))

    special = jnp.logical_or(jnp.logical_or(turns, lands), relays)
    pl.semaphore_wait(barrier, jnp.where(special, 5, 3))

    def detour(j):
        at = pl.ds(pl.multiple_of(j * CHANS, CHANS), CHANS)
        return pltpu.make_async_remote_copy(
            src_ref=own_ref.at[at], dst_ref=passing,
            send_sem=shift_send.at[j], recv_sem=pass_recv,
            device_id=(place_of(z, x, 4 - j, 1), seg), device_id_type=pl.DeviceIdType.MESH,
        )

    def forward(j):
        at = pl.ds(pl.multiple_of(j * CHANS, CHANS), CHANS)
        return pltpu.make_async_remote_copy(
            src_ref=passing, dst_ref=partner.at[at],
            send_sem=pass_send, recv_sem=shift_recv.at[j],
            device_id=target, device_id_type=pl.DeviceIdType.MESH,
        )

    def shift(j):
        at = pl.ds(pl.multiple_of(j * CHANS, CHANS), CHANS)
        return pltpu.make_async_remote_copy(
            src_ref=own_ref.at[at], dst_ref=partner.at[at],
            send_sem=shift_send.at[j], recv_sem=shift_recv.at[j],
            device_id=ahead, device_id_type=pl.DeviceIdType.MESH,
        )

    def swap(j):
        return pltpu.make_async_remote_copy(
            src_ref=send.at[j], dst_ref=got.at[j],
            send_sem=swap_send.at[j], recv_sem=swap_recv.at[j],
            device_id=opposite, device_id_type=pl.DeviceIdType.MESH,
        )

    @pl.when(turns)
    def _():
        for j in range(CHUNKS // 2, CHUNKS):
            detour(j).start()

    for j in range(CHUNKS // 2):
        shift(j).start()

    @pl.when(jnp.logical_not(turns))
    def _():
        for j in range(CHUNKS // 2, CHUNKS):
            shift(j).start()

    for j in range(CHUNKS // 2, CHUNKS):

        @pl.when(jnp.logical_and(relays, y == 4 - j))
        def _(j=j):
            detour(j).wait_recv()
            forward(j).start()

    row = lax.broadcasted_iota(jnp.int32, (GROUP, WIDE), 0)
    lane = lax.broadcasted_iota(jnp.int32, (GROUP, WIDE), 1)
    kept = jnp.where(blk > 0, 1.0, 0.0)
    mask = jnp.where(row == lane % GROUP, kept, 0.0).astype(jnp.bfloat16)
    wide_lane = lax.broadcasted_iota(jnp.int32, (CB, WIDE), 1)
    turn = jnp.where(wide_lane < WIDE // 2, -1.0, 1.0).astype(jnp.bfloat16)
    top = lax.broadcasted_iota(jnp.int32, (HALF, 256), 0) == 0

    def chunk_step(j, carry):
        shift(j).wait()
        chan = pl.ds(pl.multiple_of(j * CHANS, CHANS), CHANS)

        def one(group):
            cols = pl.ds(pl.multiple_of(group * WIDE, WIDE), WIDE)
            own = own_ref[:, cols]
            turned = jnp.concatenate([own[:, CB:], own[:, :CB]], axis=1) * turn
            spread = jnp.broadcast_to(partner[chan, cols][:, None, :], (CHANS, GROUP, WIDE))
            out = lax.dot_general(
                (spread * mask[None]).reshape(CHANS * GROUP, WIDE),
                jnp.concatenate([own, turned], 0),
                (((1,), (1,)), ((), ())),
                preferred_element_type=jnp.float32,
            ).astype(jnp.bfloat16)
            rows = pl.ds(pl.multiple_of(group * GROUP, GROUP), GROUP)
            for i in range(CHANS // 2):
                first = out[2 * i * GROUP : (2 * i + 1) * GROUP]
                second = out[(2 * i + 1) * GROUP : (2 * i + 2) * GROUP]
                pair = slice(i * WIDE, (i + 1) * WIDE)
                g_re[rows, pair] = jnp.concatenate([first[:, :CB], second[:, :CB]], 1)
                g_im[rows, pair] = jnp.concatenate([first[:, CB:], second[:, CB:]], 1)

        def body(i, carry):
            for u in range(unroll):
                one(i * unroll + u)
            return carry

        lax.fori_loop(0, GROUPS // unroll, body, 0)
        for i in range(CHUNK // 256):
            cols = slice(i * 256, (i + 1) * 256)
            even = jnp.dot(cos_ref[...], g_re[:, cols], preferred_element_type=jnp.float32)
            odd = jnp.dot(sin_ref[...], g_im[:, cols], preferred_element_type=jnp.float32)
            low, last = even[:HALF], even[HALF : HALF + 1]
            before = jnp.where(top, last, low) + odd
            after = jnp.where(top, low, low - odd)
            piece, part = j * 2 + i // 2, slice(i % 2 * 256, (i % 2 + 1) * 256)
            keep[piece, :, part] = jnp.where(seg == 0, before, after)
            send[piece, :, part] = jnp.where(seg == 0, after, before).astype(jnp.bfloat16)
            if i % 2 == 1:
                swap(piece).start()
        return carry

    lax.fori_loop(0, CHUNKS, chunk_step, 0)

    row_of = lax.broadcasted_iota(jnp.int32, (256, 256), 0)
    upper = jnp.where(row_of < lax.broadcasted_iota(jnp.int32, (256, 256), 1), 1.0, 0.0)
    upper = upper.astype(jnp.bfloat16)
    owner_row = lax.broadcasted_iota(jnp.int32, (STACKS_DEV, 256), 0)

    def index_step(i, carry):
        seen, named = carry
        at = pl.ds(pl.multiple_of(i * 256, 256), 256)
        owner = owner_ref[:, at]
        ordered = owner % 2 * CB + owner // 2
        hot = jnp.where(owner_row == ordered, 1.0, 0.0)
        before = jnp.dot(hot.astype(jnp.bfloat16), upper, preferred_element_type=jnp.float32) + seen
        position = jnp.sum(hot * before, axis=0, keepdims=True).astype(jnp.int32)
        dest_ref[:, at] = ordered * CAP + position
        names = jnp.where(owner_row // 2 == position, (slot_ref[:, at] + 1).astype(jnp.float32), 0.0)
        named += lax.dot_general(
            hot.astype(jnp.bfloat16),
            names.astype(jnp.bfloat16),
            (((1,), (1,)), ((), ())),
            preferred_element_type=jnp.float32,
        )
        return seen + jnp.sum(hot, axis=1, keepdims=True), named

    _, named = lax.fori_loop(
        0,
        PAIRS // 256,
        index_step,
        (jnp.zeros((STACKS_DEV, 1), jnp.float32), jnp.zeros((STACKS_DEV, STACKS_DEV), jnp.float32)),
    )
    slots_ref[...] = named.astype(jnp.int32) - 1

    def finish_step(j, carry):
        swap(j).wait()
        for i in range(2):
            cols = slice(i * 256, (i + 1) * 256)
            turned = (keep[j, :, cols] + got[j, :, cols].astype(jnp.float32)).T
            for side in range(2):
                at = pl.ds((j * 2 + i) * 512 + side, 256, stride=2)
                rows_ref[at, :] = turned[:, side * WIDE : (side + 1) * WIDE]
        return carry

    lax.fori_loop(0, 2 * CHUNKS, finish_step, 0)
    for j in range(CHUNKS // 2, CHUNKS):

        @pl.when(jnp.logical_and(relays, y == 4 - j))
        def _(j=j):
            forward(j).wait_send()


def tile_rows(own, cos_rows, sin_rows, owner, slot):
    return pl.pallas_call(
        tile_kernel,
        out_shape=(
            jax.ShapeDtypeStruct((2 * PAIRS, WIDE), jnp.float32),
            jax.ShapeDtypeStruct((1, PAIRS), jnp.int32),
            jax.ShapeDtypeStruct((STACKS_DEV, STACKS_DEV), jnp.int32),
        ),
        in_specs=[VMEM] * 5,
        out_specs=(VMEM, VMEM, VMEM),
        scratch_shapes=[
            pltpu.VMEM((CB, GROUPS * WIDE), jnp.bfloat16),
            pltpu.VMEM((F, CHUNK), jnp.bfloat16),
            pltpu.VMEM((F, CHUNK), jnp.bfloat16),
            pltpu.VMEM((2 * CHUNKS, HALF, CHUNK // 2), jnp.float32),
            pltpu.VMEM((2 * CHUNKS, HALF, CHUNK // 2), jnp.bfloat16),
            pltpu.VMEM((2 * CHUNKS, HALF, CHUNK // 2), jnp.bfloat16),
            pltpu.VMEM((CHANS, GROUPS * WIDE), jnp.bfloat16),
            pltpu.SemaphoreType.DMA((CHUNKS,)),
            pltpu.SemaphoreType.DMA((CHUNKS,)),
            pltpu.SemaphoreType.DMA((2 * CHUNKS,)),
            pltpu.SemaphoreType.DMA((2 * CHUNKS,)),
            pltpu.SemaphoreType.DMA,
            pltpu.SemaphoreType.DMA,
        ],
        compiler_params=pltpu.CompilerParams(
            collective_id=2, has_side_effects=True, vmem_limit_bytes=40 * 2**20
        ),
        cost_estimate=pl.CostEstimate(
            flops=25_000_000_000, bytes_accessed=2**24, transcendentals=0
        ),
        name="tiles",
    )(own, cos_rows, sin_rows, owner, slot)


def place_kernel(dest_ref, rows, out_ref, spread):
    def clear(i, carry):
        spread[pl.ds(pl.multiple_of(i * 512, 512), 512), :] = jnp.zeros((512, WIDE), jnp.float32)
        return carry

    lax.fori_loop(0, spread.shape[0] // 512, clear, 0)

    def move(i, carry):
        for u in range(64):
            p = i * 64 + u
            to = pl.multiple_of(dest_ref[p] * 2, 2)
            spread[pl.ds(to, 2), :] = rows[pl.ds(pl.multiple_of(p * 2, 2), 2), :]
        return carry

    lax.fori_loop(0, PAIRS // 64, move, 0)

    def finish(i, carry):
        at = pl.ds(pl.multiple_of(i * 512, 512), 512)
        out_ref[at, :] = spread[at, :].astype(jnp.bfloat16)
        return carry

    lax.fori_loop(0, spread.shape[0] // 512, finish, 0)


def place_rows(dest, rows, rows_out):
    return pl.pallas_call(
        place_kernel,
        out_shape=jax.ShapeDtypeStruct((2 * rows_out, WIDE), jnp.bfloat16),
        in_specs=[SMEM, VMEM],
        out_specs=VMEM,
        scratch_shapes=[pltpu.VMEM((2 * rows_out, WIDE), jnp.float32)],
        compiler_params=pltpu.CompilerParams(vmem_limit_bytes=24 * 2**20),
        name="place",
    )(dest, rows)


SLOTS_A, SLOTS_C, SLOTS_B = 48, 48, 32
AC = SLOTS_A + SLOTS_C


def reduce_kernel(
    rows_ref, slots_ref, out_ref,
    sib_rows, sib_slots, da, db, dc, ra, rb, rc, sa, sb, sc, ra2, rb2, rc2, t, tb, rt, rtb,
    send_sem, recv_sem,
):
    blk = lax.axis_index("blk")
    seg = lax.axis_index("seg")
    core = blk % 2
    y = (blk // 2) % 4
    x = (blk // 8) % 2
    z = blk // 16
    other = (place_of(z, x, y, 1 - core), seg)
    across = (place_of(z, 1 - x, y, core), seg)

    def along_y(k):
        return (place_of(z, x, (y + k) % 4, core), seg)

    def along_z(k):
        return (place_of((z + k) % 8, x, y, core), seg)

    partners = [other, across] + [along_y(k) for k in (1, 2, 3)] + [along_z(k) for k in range(1, 8)]
    barrier = pltpu.get_barrier_semaphore()
    for partner in partners:
        pl.semaphore_signal(barrier, inc=1, device_id=partner, device_id_type=pl.DeviceIdType.MESH)
    pl.semaphore_wait(barrier, len(partners))
    used = [0]

    def copy(src, dst, device):
        i = used[0]
        used[0] += 1
        made = pltpu.make_async_remote_copy(
            src_ref=src, dst_ref=dst, send_sem=send_sem.at[i], recv_sem=recv_sem.at[i],
            device_id=device, device_id_type=pl.DeviceIdType.MESH,
        )
        made.start()
        return made

    half = 2 * CB * CAP
    span = 2 * CAP
    order = [4, 3, 5, 2, 6, 1, 7, 0]
    named = copy(slots_ref.at[pl.ds((1 - core) * CB, CB)], sib_slots, other)
    swaps = {}
    for k in order:
        first = (z + k) % 8 * (8 * span)
        swaps[k] = copy(
            rows_ref.at[pl.ds((1 - core) * half + first, 8 * span)],
            sib_rows.at[pl.ds(first, 8 * span)],
            other,
        )
    named.wait()
    lane = lax.broadcasted_iota(jnp.int32, (1, 4 * CAP), 1)
    slot = lax.broadcasted_iota(jnp.int32, (STACKS_DEV, 4 * CAP), 0)

    def dense_one(i):
        zz, xx, yy = i // 8, (i // 4) % 2, i % 4
        names = jnp.concatenate([slots_ref[pl.ds(core * CB + i, 1), :], sib_slots[pl.ds(i, 1), :]], 1)
        left = jnp.where(lane % 2 == 0, names, -1)
        right = jnp.where(lane % 2 == 1, names, -1)
        hot = jnp.concatenate([slot == left, slot == right], 0)
        mine = rows_ref[pl.ds(pl.multiple_of(core * half + i * span, span), span), :]
        theirs = sib_rows[pl.ds(pl.multiple_of(i * span, span), span), :]
        total = jnp.dot(
            jnp.where(hot, 1.0, 0.0).astype(jnp.bfloat16),
            jnp.concatenate([mine, theirs], 0),
            preferred_element_type=jnp.float32,
        ).astype(jnp.bfloat16)
        total = jnp.concatenate([total[:STACKS_DEV], total[STACKS_DEV:]], 1)
        da[yy, zz, xx] = total[:SLOTS_A]
        dc[xx, zz, yy] = total[SLOTS_A:AC]
        db[zz, xx * 4 + yy] = total[AC:]

    def wide(value):
        return value.astype(jnp.float32)

    first_a, first_b, first_c, second_a, second_c, third = {}, {}, {}, {}, {}, {}
    for k in order:
        swaps[k].wait()
        there = (z + k) % 8

        def dense(i, carry, there=there):
            for u in range(4):
                dense_one(there * 8 + i * 4 + u)
            return carry

        lax.fori_loop(0, 2, dense, 0)
        first_c[k] = copy(dc.at[1 - x, there], rc.at[there], across)
        first_a[k] = [
            copy(da.at[(y + j) % 4, there], ra.at[j - 1, there], along_y(j)) for j in (2, 1, 3)
        ]
        if k:
            first_b[k] = copy(db.at[there], rb.at[k - 1], along_z(k))

    def second(k):
        there = (z + k) % 8
        first_c[k].wait()

        def sum_c(i, carry):
            sc[i, there] = (wide(dc[x, there, i]) + wide(rc[there, i])).astype(jnp.bfloat16)
            return carry

        lax.fori_loop(0, 4, sum_c, 0)
        second_c[k] = [
            copy(sc.at[(y + j) % 4, there], rc2.at[j - 1, there], along_y(j)) for j in (2, 1, 3)
        ]
        for made in first_a[k]:
            made.wait()

        def sum_a(i, carry):
            total = wide(da[y, there, i])
            for j in range(3):
                total += wide(ra[j, there, i])
            sa[i, there] = total.astype(jnp.bfloat16)
            return carry

        lax.fori_loop(0, 2, sum_a, 0)
        second_a[k] = copy(sa.at[1 - x, there], ra2.at[there], across)

    def finish(k):
        there = (z + k) % 8
        second_a[k].wait()
        t[there, :SLOTS_A] = (wide(sa[x, there]) + wide(ra2[there])).astype(jnp.bfloat16)
        for made in second_c[k]:
            made.wait()
        total = wide(sc[y, there])
        for j in range(3):
            total += wide(rc2[j, there])
        t[there, SLOTS_A:] = total.astype(jnp.bfloat16)
        if k:
            third[k] = copy(t.at[there], rt.at[k - 1], along_z(k))

    late = 2
    for n, k in enumerate(order):
        second(k)
        if n >= late:
            finish(order[n - late])
    for made in first_b.values():
        made.wait()

    def sum_b(i, carry):
        total = wide(db[z, i])
        for k in range(7):
            total += wide(rb[k, i])
        sb[i % 4, i // 4] = total.astype(jnp.bfloat16)
        return carry

    lax.fori_loop(0, 8, sum_b, 0)
    second_b = [copy(sb.at[(y + k) % 4], rb2.at[k - 1], along_y(k)) for k in (1, 2, 3)]
    for k in order[-late:]:
        finish(k)
    for made in second_b:
        made.wait()

    def sum_b2(i, carry):
        total = wide(sb[y, i])
        for k in range(3):
            total += wide(rb2[k, i])
        tb[i] = total.astype(jnp.bfloat16)
        return carry

    lax.fori_loop(0, 2, sum_b2, 0)
    third_b = copy(tb.at[1 - x], rtb, across)
    total = wide(t[z])
    for k in order[:-1]:
        third[k].wait()
        total += wide(rt[k - 1])
    out_ref[:AC, :] = total
    third_b.wait()
    out_ref[AC:, :] = wide(tb[x]) + wide(rtb[...])


def reduce_rows(rows, slots):
    def buf(*shape):
        return pltpu.VMEM((*shape, HALF), jnp.bfloat16)

    a, b, c = SLOTS_A, SLOTS_B, SLOTS_C
    count = 9 + 8 + 24 + 7 + 24 + 8 + 7 + 3 + 1
    return pl.pallas_call(
        reduce_kernel,
        out_shape=jax.ShapeDtypeStruct((STACKS_DEV, HALF), jnp.float32),
        in_specs=[VMEM, VMEM],
        out_specs=VMEM,
        scratch_shapes=[
            pltpu.VMEM((2 * CB * CAP, WIDE), jnp.bfloat16), pltpu.VMEM((CB, STACKS_DEV), jnp.int32),
            buf(4, 8, 2, a), buf(8, 8, b), buf(2, 8, 4, c), buf(3, 8, 2, a), buf(7, 8, b), buf(8, 4, c),
            buf(2, 8, a), buf(4, 2, b), buf(4, 8, c), buf(8, a), buf(3, 2, b), buf(3, 8, c),
            buf(8, AC), buf(2, b), buf(7, AC), buf(b),
            pltpu.SemaphoreType.DMA((count,)), pltpu.SemaphoreType.DMA((count,)),
        ],
        compiler_params=pltpu.CompilerParams(
            collective_id=1, has_side_effects=True, vmem_limit_bytes=40 * 2**20
        ),
        cost_estimate=pl.CostEstimate(flops=2_000_000_000, bytes_accessed=2**23, transcendentals=0),
        name="reduce_rows",
    )(rows, slots)


def local(spectra, owner_device, stack_slot):
    blk_devices = lax.axis_size("blk")
    seg = lax.axis_index("seg")
    factor = (2.0 * F * SEGS) ** (-0.5)
    cos_rows, sin_rows = lag_rows(factor)
    rows, dest, slots = tile_rows(
        whiten(spectra),
        cos_rows,
        sin_rows,
        owner_device.reshape(1, PAIRS),
        stack_slot.reshape(1, PAIRS),
    )
    outgoing = place_rows(dest.reshape(PAIRS), rows, blk_devices * CAP)
    stacks = reduce_rows(outgoing, slots)
    lags = lax.iota(jnp.int32, HALF)
    turned = jnp.roll(stacks[:, ::-1], 1, axis=1)
    stacks = jnp.where(seg == 0, turned, stacks)
    return stacks.astype(jnp.bfloat16)


def solution(mesh):
    placed = (P("seg", "blk", None, None), P("blk", None), P("blk"))
    return jax.shard_map(
        local, mesh=mesh, in_specs=placed, out_specs=P("blk", "seg"), check_vma=False
    )
```
